1024 devices in a mesh: chan: 16 (over x, y_hi), ctx: 64 (over z, y_lo, core).
Axes of the slice: x: 8, y: 8 (y_hi: 2, y_lo: 4; y = y_hi * 4 + y_lo), z: 8, core: 2. Of those that a mesh axis runs over, the one named last changes fastest.
Arguments:
- short_query: bfloat16 [4096, 65536], P('chan', 'ctx'), may hold values from -6 to 6
- short_key: bfloat16 [4096, 65536], P('chan', 'ctx'), may hold values from -6 to 6
- short_value: bfloat16 [4096, 65536], P('chan', 'ctx'), may hold values from -6 to 6
- long_query: bfloat16 [4096, 65536], P('chan', 'ctx'), may hold values from -6 to 6
- long_key: bfloat16 [4096, 65536], P('chan', 'ctx'), may hold values from -6 to 6
- short_taps: bfloat16 [256, 128], P('chan'), may hold values from -0.5 to 0.5
- long_residue: float32 [256, 16], P('chan'), may hold values from -2 to 2
- long_rate: float32 [256, 16], P('chan'), may hold values from 3e-06 to 0.05
Outputs:
- block_output: bfloat16 [4096, 65536], P('chan', 'ctx')
The draws below stay inside these ranges and needn't reach their ends.
All inputs are finite; a program needn't handle non-finite values.
Results may differ from the reference program's by a relative error of at most 0.015.
Values may be sent and summed in bfloat16 or wider, within the bound.
A program may use at most 64 MiB of HBM per device.

```python
import math
import jax
import jax.numpy as jnp
from jax import lax

D = 4096
TAPS = 128
MODES = 16
FGROUP = 16
SPAN = 512
TOKENS = 65536
GROUPS = 256
N_CTX = 64


def steps_of(own_key, dims, shards, low, high):
    factor_of = 1.0
    for axis_at, blocks in shards:
        steps = jax.random.uniform(jax.random.fold_in(jax.random.fold_in(own_key, 6), axis_at), (blocks,), jnp.float32, low / len(shards), high / len(shards))
        factor_of = factor_of * jnp.repeat(jnp.exp(steps), dims[axis_at] // blocks).reshape((-1,) + (1,) * (len(dims) - 1 - axis_at))
    return factor_of


def scatter_about(key, dims, scale, most, cuts=(), kind=jnp.bfloat16):
    level = steps_of(key, dims, cuts, -0.22, 0.18) if cuts else 1.0
    values = jax.random.normal(key, dims, jnp.float32) * scale * level
    return jnp.minimum(jnp.maximum(values, -most), most).astype(kind)


def setup_inputs(seed: int = 0) -> dict:
    key_of = jax.random.split(jax.random.key(seed), 9)
    return {
        "short_query": scatter_about(key_of[0], (D, TOKENS), 1.0, 6.0, ((0, 16), (1, 64))),
        "short_key": scatter_about(key_of[1], (D, TOKENS), 1.0, 6.0, ((0, 16), (1, 64))),
        "short_value": scatter_about(key_of[2], (D, TOKENS), 1.0, 6.0, ((0, 16), (1, 64))),
        "long_query": scatter_about(key_of[3], (D, TOKENS), 1.0, 6.0, ((0, 16), (1, 64))),
        "long_key": scatter_about(key_of[4], (D, TOKENS), 1.0, 6.0, ((0, 16), (1, 64))),
        "short_taps": scatter_about(key_of[5], (GROUPS, TAPS), TAPS ** -0.5, 0.5, ((0, 16),)),
        "long_residue": scatter_about(key_of[6], (GROUPS, MODES), 0.35, 2.0, ((0, 16),), jnp.float32),
        "long_rate": jnp.clip(jnp.exp(math.log(0.05) - 9.721166 * jax.random.uniform(key_of[7], (GROUPS, MODES), jnp.float32) ** steps_of(key_of[7], (GROUPS, MODES), ((0, 16),), -0.2, 0.2)), 3.000000106112566e-06, 0.05),
    }


def to_natural(stored):
    split = stored.reshape(stored.shape[0], N_CTX, 2, SPAN)
    first = split[:, :, 0].reshape(stored.shape[0], N_CTX * SPAN)
    second = jnp.flip(split[:, :, 1], axis=1).reshape(stored.shape[0], N_CTX * SPAN)
    return jnp.concatenate([first, second], axis=1)

def to_stored(natural):
    blocks = natural.reshape(natural.shape[0], 2 * N_CTX, SPAN)
    paired = jnp.stack([blocks[:, :N_CTX], jnp.flip(blocks[:, N_CTX:], axis=1)], axis=2)
    return paired.reshape(natural.shape[0], TOKENS)

def fft_conv(signal, filt):
    length = signal.shape[-1]
    size = 2 * length
    spectrum = jnp.fft.rfft(signal, n=size, axis=-1) * jnp.fft.rfft(filt, n=size, axis=-1)
    return jnp.fft.irfft(spectrum, n=size, axis=-1)[..., :length].astype(jnp.float32)

def reference(short_query, short_key, short_value, long_query, long_key, short_taps, long_residue, long_rate):
    mixed = (short_key.astype(jnp.float32) * short_value.astype(jnp.float32)).astype(jnp.bfloat16)
    grouped = to_natural(mixed).astype(jnp.float32).reshape(GROUPS, FGROUP, TOKENS)

    def short_group(packed):
        return fft_conv(packed[0], packed[1][None, :])
    short_conv = lax.map(short_group, (grouped, short_taps.astype(jnp.float32))).reshape(D, TOKENS)
    query_nat = to_natural(short_query).astype(jnp.float32)
    key_nat = to_natural(long_key).astype(jnp.float32)
    long_input = (key_nat * (query_nat * short_conv)).astype(jnp.bfloat16)
    positions = jnp.arange(TOKENS, dtype=jnp.float32)

    def long_group(packed):
        signal, residue, rate = packed
        filt = lax.optimization_barrier(jnp.sum((residue * jnp.sqrt(rate))[:, None] * jnp.exp(-rate[:, None] * positions[None, :]), axis=0))
        return fft_conv(signal, filt[None, :])
    long_conv = lax.map(long_group, (long_input.astype(jnp.float32).reshape(GROUPS, FGROUP, TOKENS), long_residue, long_rate)).reshape(D, TOKENS)
    output = (to_natural(long_query).astype(jnp.float32) * long_conv).astype(jnp.bfloat16)
    return to_stored(output)
```

```python
import functools

import jax
import jax.numpy as jnp
from jax import lax
from jax.experimental import pallas as pl
from jax.experimental.pallas import tpu as pltpu
from jax.sharding import PartitionSpec as P

TAPS = 128
FGROUP = 16
MODES = 16
CHUNK = 256
RING = 8
LANES = 128
MESH = pl.DeviceIdType.MESH
F32 = jnp.float32
BF16 = jnp.bfloat16


def dot(a, b):
    return lax.dot_general(a, b, (((1,), (0,)), ((), ())), preferred_element_type=F32)


def dot_t(a, b):
    return lax.dot_general(a, b, (((1,), (1,)), ((), ())), preferred_element_type=F32)


def split_float(values):
    high = values.astype(BF16)
    low = (values - high.astype(F32)).astype(BF16)
    return high, low


def iota(shape, axis):
    return lax.broadcasted_iota(jnp.int32, shape, axis)


def kernel(
    n_ctx,
    sq_hbm,
    sk_hbm,
    sv_hbm,
    lq_hbm,
    lk_hbm,
    taps_hbm,
    res_hbm,
    rate_hbm,
    out,
    sq,
    sk,
    sv,
    lq,
    lk,
    taps,
    res,
    rate,
    mixed,
    tails,
    halo,
    first,
    upper_w,
    taps_f,
    pad,
    fe,
    gt,
    filt,
    x,
    y,
    ends,
    e_out,
    e_in,
    p_out,
    p_in,
    s_out,
    s_in,
    coef,
    load_sem,
    halo_send,
    halo_recv,
    a_send,
    a_recv,
    b_send,
    b_recv,
    c_send,
    c_recv,
):
    chans, length = sk.shape
    half = length // 2
    groups = chans // FGROUP
    nz = n_ctx // RING
    me = lax.axis_index("ctx")
    plane = lax.div(me, RING)
    place = lax.rem(me, RING)
    after = lax.rem(me + 1, n_ctx)
    before = lax.rem(me + n_ctx - 1, n_ctx)

    def in_plane(k):
        return plane * RING + lax.rem(place + k, RING)

    def in_column(k):
        return lax.rem(plane + k, nz) * RING + place

    def load(n, src, dst):
        copy = pltpu.make_async_copy(src, dst, load_sem.at[n])
        copy.start()
        return copy

    tail_cols = ((half - TAPS, half), (length - TAPS, length))
    body_cols = ((0, half - TAPS), (half, length - TAPS))
    tail_loads = []
    for b, (lo, hi) in enumerate(tail_cols):
        tail_loads.append(load(2 * b, sk_hbm.at[:, lo:hi], sk.at[:, lo:hi]))
        tail_loads.append(load(2 * b + 1, sv_hbm.at[:, lo:hi], sv.at[:, lo:hi]))
    rate_load = load(4, rate_hbm, rate)
    res_load = load(5, res_hbm, res)
    taps_load = load(6, taps_hbm, taps)
    body_loads = []
    for b, (lo, hi) in enumerate(body_cols):
        body_loads.append(load(7 + 2 * b, sk_hbm.at[:, lo:hi], sk.at[:, lo:hi]))
        body_loads.append(load(8 + 2 * b, sv_hbm.at[:, lo:hi], sv.at[:, lo:hi]))
    sq_load = load(11, sq_hbm, sq)
    lk_load = load(12, lk_hbm, lk)
    lq_load = load(13, lq_hbm, lq)

    barrier = pltpu.get_barrier_semaphore()
    partners = [before, after]
    partners += [in_plane(k) for k in range(1, RING)]
    partners += [in_column(k) for k in range(1, nz)]
    for partner in partners:
        pl.semaphore_signal(
            barrier, inc=1, device_id={"ctx": partner}, device_id_type=MESH
        )

    for copy in tail_loads:
        copy.wait()
    for b, (lo, hi) in enumerate(tail_cols):
        product = sk[:, lo:hi] * sv[:, lo:hi]
        mixed[:, lo:hi] = product
        tails[b] = product
    pl.semaphore_wait(barrier, len(partners))

    halo_copies = []
    for b, target in enumerate((after, before)):
        copy = pltpu.make_async_remote_copy(
            src_ref=tails.at[b],
            dst_ref=halo.at[b],
            send_sem=halo_send.at[b],
            recv_sem=halo_recv.at[b],
            device_id={"ctx": target},
            device_id_type=MESH,
        )
        copy.start()
        halo_copies.append(copy)

    rate_load.wait()
    res_load.wait()
    taps_load.wait()
    taps_f[...] = taps[...].astype(F32)

    def spread(values):
        pad[...] = jnp.zeros_like(pad)
        pad[:, 0:MODES] = values
        return pltpu.roll(pad[...], 0, 1, stride=MODES, stride_axis=0)

    rate_row = jnp.sum(spread(rate[...]), axis=0, keepdims=True)
    weight = spread(res[...] * jnp.sqrt(rate[...]))
    weight_row = jnp.sum(weight, axis=0, keepdims=True)
    steps = iota((CHUNK, LANES), 0).astype(F32)
    for h in range(2):
        r = rate_row[:, h * LANES : (h + 1) * LANES]
        high, low = split_float(jnp.exp(-r * steps))
        gt[h, :, 0:LANES] = high
        gt[h, :, LANES:] = low
        high, low = split_float(jnp.exp(-r * (CHUNK - 1.0 - steps)))
        fe[h, :, 0:LANES] = high
        fe[h, :, LANES:] = low

    total = jnp.zeros((groups, CHUNK), F32)
    for h in range(2):
        high, low = split_float(weight[:, h * LANES : (h + 1) * LANES])
        total = total + dot_t(jnp.concatenate([high, high], axis=1), gt[h])
        total = total + dot_t(
            jnp.concatenate([low, jnp.zeros_like(low)], axis=1), gt[h]
        )
    filt[...] = total

    for copy in body_loads:
        copy.wait()
    for lo, hi in body_cols:
        mixed[:, lo:hi] = sk[:, lo:hi] * sv[:, lo:hi]
    sq_load.wait()
    lk_load.wait()

    lower_mask = iota((TAPS, TAPS), 1) >= iota((TAPS, TAPS), 0)
    blocks = length // TAPS
    firsts = (0, blocks // 2)

    def gated(rows, m, conv):
        cols = pl.ds(m * TAPS, TAPS)
        value = lk[rows, cols].astype(F32) * (sq[rows, cols].astype(F32) * conv)
        x[rows, cols] = value.astype(BF16)

    def short_group(g, _):
        rows = pl.ds(pl.multiple_of(g * FGROUP, FGROUP), FGROUP)
        line = jnp.broadcast_to(taps_f[pl.ds(g, 1), :], (TAPS, TAPS))
        skew = pltpu.roll(line, 0, 1, stride=1, stride_axis=0)
        upper = jnp.where(lower_mask, 0.0, skew).astype(BF16)
        lower = jnp.where(lower_mask, skew, 0.0).astype(BF16)
        upper_w[g] = upper
        data = []
        for m in range(blocks):
            if m in firsts:
                here = mixed[rows, m * TAPS : (m + 1) * TAPS]
                data.append(jnp.concatenate([jnp.zeros_like(here), here], axis=1))
            else:
                data.append(mixed[rows, (m - 1) * TAPS : (m + 1) * TAPS])
        conv = dot(
            jnp.concatenate(data, axis=0), jnp.concatenate([upper, lower], axis=0)
        )
        for m in range(blocks):
            part = conv[m * FGROUP : (m + 1) * FGROUP]
            if m in firsts:
                first[firsts.index(m), rows, :] = part
            else:
                gated(rows, m, part)
        return 0

    lax.fori_loop(0, groups, short_group, 0, unroll=4)

    diag = lax.div(iota((LANES, LANES), 0), FGROUP) == lax.div(
        iota((LANES, LANES), 1), MODES
    )

    def chunk_ends(chunk):
        for h in range(2):
            both = dot(
                x[h * LANES : (h + 1) * LANES, chunk * CHUNK : (chunk + 1) * CHUNK],
                fe[h],
            )
            own = jnp.where(diag, both[:, 0:LANES] + both[:, LANES:], 0.0)
            ends[chunk, :, h * LANES : (h + 1) * LANES] = jnp.sum(
                own.reshape(LANES // FGROUP, FGROUP, LANES), axis=0
            )

    chunk_ends(1)
    chunk_ends(3)

    for copy in halo_copies:
        copy.wait_recv()

    @pl.when(me == 0)
    def _():
        halo[0] = jnp.zeros_like(halo[0])

    @pl.when(me == n_ctx - 1)
    def _():
        halo[1] = tails[0]

    def first_group(g, _):
        rows = pl.ds(pl.multiple_of(g * FGROUP, FGROUP), FGROUP)
        conv = dot(
            jnp.concatenate([halo[0, rows, :], halo[1, rows, :]], axis=0), upper_w[g]
        )
        for b, m in enumerate(firsts):
            part = conv[b * FGROUP : (b + 1) * FGROUP] + first[b, rows, :]
            gated(rows, m, part)
        return 0

    lax.fori_loop(0, groups, first_group, 0, unroll=8)
    chunk_ends(0)
    chunk_ends(2)

    chunk_decay = jnp.exp(-rate_row * float(CHUNK))
    for b in range(2):
        end = ends[2 * b] * chunk_decay + ends[2 * b + 1]
        for h in range(2):
            for c in range(2):
                e_out[pl.ds(4 * b + 2 * h + c, 8, stride=8), :] = end[
                    8 * c : 8 * c + 8, h * LANES : (h + 1) * LANES
                ]

    def tile(n):
        if isinstance(n, int):
            return pl.ds(n * 8, 8)
        return pl.ds(pl.multiple_of(n * 8, 8), 8)

    def to_plane(source, target, send, recv):
        copies = []
        for k in range(1, RING):
            copy = pltpu.make_async_remote_copy(
                src_ref=source.at[tile(lax.rem(place + k, RING))],
                dst_ref=target.at[tile(place)],
                send_sem=send.at[k],
                recv_sem=recv.at[k],
                device_id={"ctx": in_plane(k)},
                device_id_type=MESH,
            )
            copy.start()
            copies.append(copy)
        return copies

    a_copies = to_plane(e_out, e_in, a_send, a_recv)
    e_in[tile(place), :] = e_out[tile(place), :]

    def inner_group(g, _):
        rows = pl.ds(pl.multiple_of(g * FGROUP, FGROUP), FGROUP)
        line = jnp.broadcast_to(filt[pl.ds(g, 1), :], (TAPS, CHUNK))
        skew = pltpu.roll(line, 0, 1, stride=1, stride_axis=0)
        near = jnp.where(lower_mask, skew[:, 0:TAPS], 0.0).astype(BF16)
        far = skew[:, TAPS:].astype(BF16)
        table = jnp.concatenate(
            [
                jnp.concatenate([near, far], axis=1),
                jnp.concatenate([jnp.zeros_like(near), near], axis=1),
            ],
            axis=0,
        )
        chunks = length // CHUNK
        data = [x[rows, c * CHUNK : (c + 1) * CHUNK] for c in range(chunks)]
        conv = dot(jnp.concatenate(data, axis=0), table)
        for c in range(chunks):
            y[rows, c * CHUNK : (c + 1) * CHUNK] = conv[
                c * FGROUP : (c + 1) * FGROUP
            ]
        return 0

    row = iota((8, LANES), 0)
    is_low = row < 4
    rate_tile = jnp.where(
        lax.rem(lax.div(row, 2), 2) == 0, rate_row[:, 0:LANES], rate_row[:, LANES:]
    )
    span_decay = jnp.exp(-rate_tile * float(half))
    for p in range(RING):
        count = jnp.where(is_low, p, RING - 1 - p).astype(F32)
        coef[p] = jnp.exp(-rate_tile * (half * count))
    for z in range(nz):
        count = jnp.where(is_low, plane - 1 - z, z - plane - 1)
        factor = jnp.exp(-rate_tile * (half * RING * jnp.maximum(count, 0).astype(F32)))
        coef[RING + z] = jnp.where(count >= 0, factor, 0.0)
        count = (2 * nz - 2 - z - plane).astype(F32)
        factor = jnp.exp(-rate_tile * (half * RING * count))
        coef[RING + nz + z] = jnp.where(is_low, 0.0, factor)

    lax.fori_loop(0, 6, inner_group, 0, unroll=3)

    for copy in a_copies:
        copy.wait_recv()
    state = jnp.zeros((8, LANES), F32)
    prefix = []
    for p in range(RING):
        prefix.append(state)
        state = state * span_decay + jnp.where(
            is_low, e_in[tile(p), :], e_in[tile(RING - 1 - p), :]
        )
    p_out[...] = state
    b_copies = []
    for k in range(1, nz):
        copy = pltpu.make_async_remote_copy(
            src_ref=p_out,
            dst_ref=p_in.at[tile(plane)],
            send_sem=b_send.at[k],
            recv_sem=b_recv.at[k],
            device_id={"ctx": in_column(k)},
            device_id_type=MESH,
        )
        copy.start()
        b_copies.append(copy)
    p_in[tile(plane), :] = state
    for p in range(RING):
        s_out[tile(p), :] = jnp.where(is_low, prefix[p], prefix[RING - 1 - p])

    lax.fori_loop(6, 11, inner_group, 0, unroll=5)

    for copy in b_copies:
        copy.wait_recv()
    carry = jnp.zeros((8, LANES), F32)
    for z in range(nz):
        total = p_in[tile(z), :]
        carry = carry + coef[RING + z] * total
        carry = carry + coef[RING + nz + z] * pltpu.roll(total, 4, 0)
    for p in range(RING):
        s_out[tile(p), :] = s_out[tile(p), :] + coef[p] * carry
    c_copies = to_plane(s_out, s_in, c_send, c_recv)
    s_in[tile(place), :] = s_out[tile(place), :]

    lax.fori_loop(11, groups, inner_group, 0, unroll=5)
    lq_load.wait()

    for copy in c_copies:
        copy.wait_recv()
    from_start = weight_row * jnp.exp(-rate_row)
    for b in range(2):
        for h in range(2):
            lanes = slice(h * LANES, (h + 1) * LANES)
            start = jnp.concatenate(
                [s_in[pl.ds(4 * b + 2 * h + c, 8, stride=8), :] for c in range(2)],
                axis=0,
            )
            rows = slice(h * LANES, (h + 1) * LANES)
            for c in range(2):
                chunk = 2 * b + c
                if c == 1:
                    start = start * chunk_decay[:, lanes] + ends[2 * b, :, lanes]
                scaled = start * from_start[:, lanes]
                tiled = jnp.concatenate([scaled] * (LANES // FGROUP), axis=0)
                states = jnp.where(diag, tiled, 0.0).astype(BF16)
                carried = dot_t(jnp.concatenate([states, states], axis=1), gt[h])
                cols = slice(chunk * CHUNK, (chunk + 1) * CHUNK)
                value = lq[rows, cols].astype(F32) * (y[rows, cols] + carried)
                out[rows, cols] = value.astype(BF16)

    for copy in halo_copies + a_copies + b_copies + c_copies:
        copy.wait_send()


def per_device(sq, sk, sv, lq, lk, taps, res, rate):
    chans, length = sk.shape
    n_ctx = lax.axis_size("ctx")
    nz = n_ctx // RING
    groups = chans // FGROUP
    wide = pltpu.VMEM((chans, length), BF16)
    message = pltpu.VMEM((8 * RING, LANES), F32)
    dma = pltpu.SemaphoreType.DMA
    scratch = [
        wide,
        wide,
        wide,
        wide,
        wide,
        pltpu.VMEM(taps.shape, BF16),
        pltpu.VMEM(res.shape, F32),
        pltpu.VMEM(rate.shape, F32),
        wide,
        pltpu.VMEM((2, chans, TAPS), BF16),
        pltpu.VMEM((2, chans, TAPS), BF16),
        pltpu.VMEM((2, chans, TAPS), F32),
        pltpu.VMEM((groups, TAPS, TAPS), BF16),
        pltpu.VMEM((groups, TAPS), F32),
        pltpu.VMEM((groups, groups * MODES), F32),
        pltpu.VMEM((2, CHUNK, 2 * LANES), BF16),
        pltpu.VMEM((2, CHUNK, 2 * LANES), BF16),
        pltpu.VMEM((groups, CHUNK), F32),
        wide,
        pltpu.VMEM((chans, length), F32),
        pltpu.VMEM((length // CHUNK, FGROUP, groups * MODES), F32),
        message,
        message,
        pltpu.VMEM((8, LANES), F32),
        pltpu.VMEM((8 * nz, LANES), F32),
        message,
        message,
        pltpu.VMEM((RING + 2 * nz, 8, LANES), F32),
        dma((14,)),
        dma((2,)),
        dma((2,)),
        dma((RING,)),
        dma((RING,)),
        dma((nz,)),
        dma((nz,)),
        dma((RING,)),
        dma((RING,)),
    ]
    in_hbm = pl.BlockSpec(memory_space=pltpu.HBM)
    return pl.pallas_call(
        functools.partial(kernel, n_ctx),
        out_shape=jax.ShapeDtypeStruct((chans, length), BF16),
        in_specs=[in_hbm] * 8,
        out_specs=pl.BlockSpec(memory_space=pltpu.VMEM),
        scratch_shapes=scratch,
        compiler_params=pltpu.CompilerParams(
            collective_id=0, has_side_effects=True, vmem_limit_bytes=53 << 20
        ),
    )(sq, sk, sv, lq, lk, taps, res, rate)


def solution(mesh):
    in_specs = (P("chan", "ctx"),) * 5 + (P("chan", None),) * 3
    return jax.shard_map(
        per_device,
        mesh=mesh,
        in_specs=in_specs,
        out_specs=P("chan", "ctx"),
        check_vma=False,
    )
```

```python
import functools

import jax
import jax.numpy as jnp
from jax import lax
from jax.experimental import pallas as pl
from jax.experimental.pallas import tpu as pltpu
from jax.sharding import PartitionSpec as P

TAPS = 128
FGROUP = 16
MODES = 16
CHUNK = 256
RING = 8
LANES = 128
MESH = pl.DeviceIdType.MESH
F32 = jnp.float32
BF16 = jnp.bfloat16


def dot(a, b):
    return lax.dot_general(a, b, (((1,), (0,)), ((), ())), preferred_element_type=F32)


def dot_t(a, b):
    return lax.dot_general(a, b, (((1,), (1,)), ((), ())), preferred_element_type=F32)


def split_float(values):
    high = values.astype(BF16)
    low = (values - high.astype(F32)).astype(BF16)
    return high, low


def iota(shape, axis):
    return lax.broadcasted_iota(jnp.int32, shape, axis)


def kernel(
    n_ctx,
    sq_hbm,
    sk_hbm,
    sv_hbm,
    lk_hbm,
    taps_hbm,
    res_hbm,
    rate_hbm,
    conv_hbm,
    sq,
    sk,
    sv,
    lk,
    taps,
    res,
    rate,
    mixed,
    tails,
    halo,
    first,
    upper_w,
    taps_f,
    pad,
    fe,
    gt,
    filt,
    x,
    y,
    ends,
    from_z,
    z_out,
    z_in,
    a_out,
    a_in,
    b_out,
    b_in,
    conv,
    load_sem,
    halo_send,
    halo_recv,
    z_send,
    z_recv,
    a_send,
    a_recv,
    b_send,
    b_recv,
    conv_sem,
):
    chans, length = sk.shape
    half = length // 2
    groups = chans // FGROUP
    nz = n_ctx // RING
    me = lax.axis_index("ctx")
    plane = lax.div(me, RING)
    place = lax.rem(me, RING)
    after = lax.rem(me + 1, n_ctx)
    before = lax.rem(me + n_ctx - 1, n_ctx)

    def in_plane(k):
        return plane * RING + lax.rem(place + k, RING)

    def in_column(k):
        return lax.rem(plane + k, nz) * RING + place

    def load(n, src, dst):
        copy = pltpu.make_async_copy(src, dst, load_sem.at[n])
        copy.start()
        return copy

    tail_cols = ((half - TAPS, half), (length - TAPS, length))
    body_cols = ((0, half - TAPS), (half, length - TAPS))
    tail_loads = []
    for b, (lo, hi) in enumerate(tail_cols):
        tail_loads.append(load(2 * b, sk_hbm.at[:, lo:hi], sk.at[:, lo:hi]))
        tail_loads.append(load(2 * b + 1, sv_hbm.at[:, lo:hi], sv.at[:, lo:hi]))
    rate_load = load(4, rate_hbm, rate)
    res_load = load(5, res_hbm, res)
    taps_load = load(6, taps_hbm, taps)
    body_loads = []
    for b, (lo, hi) in enumerate(body_cols):
        body_loads.append(load(7 + 2 * b, sk_hbm.at[:, lo:hi], sk.at[:, lo:hi]))
        body_loads.append(load(8 + 2 * b, sv_hbm.at[:, lo:hi], sv.at[:, lo:hi]))
    sq_load = load(11, sq_hbm, sq)
    lk_load = load(12, lk_hbm, lk)

    barrier = pltpu.get_barrier_semaphore()
    partners = [before, after]
    partners += [in_plane(k) for k in range(1, RING)]
    partners += [in_column(k) for k in range(1, nz)]
    for partner in partners:
        pl.semaphore_signal(
            barrier, inc=1, device_id={"ctx": partner}, device_id_type=MESH
        )

    for copy in tail_loads:
        copy.wait()
    for b, (lo, hi) in enumerate(tail_cols):
        product = sk[:, lo:hi] * sv[:, lo:hi]
        mixed[:, lo:hi] = product
        tails[b] = product
    pl.semaphore_wait(barrier, len(partners))

    halo_copies = []
    for b, target in enumerate((after, before)):
        copy = pltpu.make_async_remote_copy(
            src_ref=tails.at[b],
            dst_ref=halo.at[b],
            send_sem=halo_send.at[b],
            recv_sem=halo_recv.at[b],
            device_id={"ctx": target},
            device_id_type=MESH,
        )
        copy.start()
        halo_copies.append(copy)

    rate_load.wait()
    res_load.wait()
    taps_load.wait()
    taps_f[...] = taps[...].astype(F32)

    def spread(values):
        pad[...] = jnp.zeros_like(pad)
        pad[:, 0:MODES] = values
        return pltpu.roll(pad[...], 0, 1, stride=MODES, stride_axis=0)

    rate_row = jnp.sum(spread(rate[...]), axis=0, keepdims=True)
    weight = spread(res[...] * jnp.sqrt(rate[...]))
    weight_row = jnp.sum(weight, axis=0, keepdims=True)
    steps = iota((CHUNK, LANES), 0).astype(F32)
    for h in range(2):
        r = rate_row[:, h * LANES : (h + 1) * LANES]
        high, low = split_float(jnp.exp(-r * steps))
        gt[h, :, 0:LANES] = high
        gt[h, :, LANES:] = low
        high, low = split_float(jnp.exp(-r * (CHUNK - 1.0 - steps)))
        fe[h, :, 0:LANES] = high
        fe[h, :, LANES:] = low

    total = jnp.zeros((groups, CHUNK), F32)
    for h in range(2):
        high, low = split_float(weight[:, h * LANES : (h + 1) * LANES])
        total = total + dot_t(jnp.concatenate([high, high], axis=1), gt[h])
        total = total + dot_t(
            jnp.concatenate([low, jnp.zeros_like(low)], axis=1), gt[h]
        )
    filt[...] = total

    for copy in body_loads:
        copy.wait()
    for lo, hi in body_cols:
        mixed[:, lo:hi] = sk[:, lo:hi] * sv[:, lo:hi]
    sq_load.wait()
    lk_load.wait()

    lower_mask = iota((TAPS, TAPS), 1) >= iota((TAPS, TAPS), 0)
    blocks = length // TAPS
    firsts = (0, blocks // 2)

    def gated(rows, m, conv):
        cols = pl.ds(m * TAPS, TAPS)
        value = lk[rows, cols].astype(F32) * (sq[rows, cols].astype(F32) * conv)
        x[rows, cols] = value.astype(BF16)

    def short_group(g, _):
        rows = pl.ds(pl.multiple_of(g * FGROUP, FGROUP), FGROUP)
        line = jnp.broadcast_to(taps_f[pl.ds(g, 1), :], (TAPS, TAPS))
        skew = pltpu.roll(line, 0, 1, stride=1, stride_axis=0)
        upper = jnp.where(lower_mask, 0.0, skew).astype(BF16)
        lower = jnp.where(lower_mask, skew, 0.0).astype(BF16)
        upper_w[g] = upper
        data = []
        for m in range(blocks):
            if m in firsts:
                here = mixed[rows, m * TAPS : (m + 1) * TAPS]
                data.append(jnp.concatenate([jnp.zeros_like(here), here], axis=1))
            else:
                data.append(mixed[rows, (m - 1) * TAPS : (m + 1) * TAPS])
        short = dot(
            jnp.concatenate(data, axis=0), jnp.concatenate([upper, lower], axis=0)
        )
        for m in range(blocks):
            part = short[m * FGROUP : (m + 1) * FGROUP]
            if m in firsts:
                first[firsts.index(m), rows, :] = part
            else:
                gated(rows, m, part)
        return 0

    lax.fori_loop(0, groups, short_group, 0, unroll=4)

    diag = lax.div(iota((LANES, LANES), 0), FGROUP) == lax.div(
        iota((LANES, LANES), 1), MODES
    )

    def chunk_ends(chunk):
        for h in range(2):
            both = dot(
                x[h * LANES : (h + 1) * LANES, chunk * CHUNK : (chunk + 1) * CHUNK],
                fe[h],
            )
            own = jnp.where(diag, both[:, 0:LANES] + both[:, LANES:], 0.0)
            ends[chunk, :, h * LANES : (h + 1) * LANES] = jnp.sum(
                own.reshape(LANES // FGROUP, FGROUP, LANES), axis=0
            )

    chunk_ends(1)
    chunk_ends(3)

    for copy in halo_copies:
        copy.wait_recv()

    @pl.when(me == 0)
    def _():
        halo[0] = jnp.zeros_like(halo[0])

    @pl.when(me == n_ctx - 1)
    def _():
        halo[1] = tails[0]

    def first_group(g, _):
        rows = pl.ds(pl.multiple_of(g * FGROUP, FGROUP), FGROUP)
        short = dot(
            jnp.concatenate([halo[0, rows, :], halo[1, rows, :]], axis=0), upper_w[g]
        )
        for b, m in enumerate(firsts):
            part = short[b * FGROUP : (b + 1) * FGROUP] + first[b, rows, :]
            gated(rows, m, part)
        return 0

    lax.fori_loop(0, groups, first_group, 0, unroll=8)
    chunk_ends(0)
    chunk_ends(2)

    chunk_decay = jnp.exp(-rate_row * float(CHUNK))
    end_a = ends[0] * chunk_decay + ends[1]
    end_b = ends[2] * chunk_decay + ends[3]
    powers = iota((RING, groups * MODES), 0).astype(F32)
    by_block = jnp.exp(-rate_row * (powers * half))
    powers = iota((nz, groups * MODES), 0).astype(F32)
    by_plane = jnp.exp(-rate_row * (powers * (half * RING)))

    def over_blocks(count):
        return jnp.exp(-rate_row * (half * count.astype(F32)))

    both = end_b + end_a * over_blocks(2 * n_ctx - 1 - 2 * me)
    z_out[0] = end_a.astype(BF16)
    z_out[1] = both.astype(BF16)

    def send(source, target, k, send_sem, recv_sem, device):
        copy = pltpu.make_async_remote_copy(
            src_ref=source,
            dst_ref=target.at[k],
            send_sem=send_sem.at[k],
            recv_sem=recv_sem.at[k],
            device_id={"ctx": device},
            device_id_type=MESH,
        )
        copy.start()
        return copy

    z_copies = [
        send(z_out.at[lax.div(plane + k, nz)], z_in, k, z_send, z_recv, in_column(k))
        for k in range(1, nz)
    ]

    def inner_group(g, _):
        rows = pl.ds(pl.multiple_of(g * FGROUP, FGROUP), FGROUP)
        line = jnp.broadcast_to(filt[pl.ds(g, 1), :], (TAPS, CHUNK))
        skew = pltpu.roll(line, 0, 1, stride=1, stride_axis=0)
        near = jnp.where(lower_mask, skew[:, 0:TAPS], 0.0).astype(BF16)
        far = skew[:, TAPS:].astype(BF16)
        table = jnp.concatenate(
            [
                jnp.concatenate([near, far], axis=1),
                jnp.concatenate([jnp.zeros_like(near), near], axis=1),
            ],
            axis=0,
        )
        chunks = length // CHUNK
        data = [x[rows, c * CHUNK : (c + 1) * CHUNK] for c in range(chunks)]
        inner = dot(jnp.concatenate(data, axis=0), table)
        for c in range(chunks):
            y[rows, c * CHUNK : (c + 1) * CHUNK] = inner[
                c * FGROUP : (c + 1) * FGROUP
            ]
        return 0

    lax.fori_loop(0, 6, inner_group, 0, unroll=3)

    def from_planes(first_half):
        from_z[...] = jnp.zeros_like(from_z)
        for k in range(1, nz):
            power = k - 1 if first_half else nz - 1 - k

            @pl.when((plane >= k) if first_half else (plane < k))
            def _():
                z_copies[k - 1].wait_recv()
                from_z[...] += by_plane[power : power + 1] * z_in[k].astype(F32)

        return from_z[...]

    one_plane = by_plane[1:2]
    before_a = from_planes(True)
    a_out[0] = (before_a * one_plane + end_a).astype(BF16)
    a_out[1] = before_a.astype(BF16)
    a_copies = [
        send(a_out.at[lax.div(place + k, RING)], a_in, k, a_send, a_recv, in_plane(k))
        for k in range(1, RING)
    ]
    before_b = from_planes(False)
    b_out[0] = before_b.astype(BF16)
    b_out[1] = (before_b * one_plane + both).astype(BF16)
    b_copies = [
        send(b_out.at[lax.div(place + k, RING)], b_in, k, b_send, b_recv, in_plane(k))
        for k in range(1, RING)
    ]

    lax.fori_loop(6, groups, inner_group, 0, unroll=5)

    from_start = weight_row * jnp.exp(-rate_row)
    conv_copies = []

    def finish(b, start):
        for h in range(2):
            lanes = slice(h * LANES, (h + 1) * LANES)
            rows = slice(h * LANES, (h + 1) * LANES)
            state = start[:, lanes]
            for c in range(2):
                chunk = 2 * b + c
                if c == 1:
                    state = state * chunk_decay[:, lanes] + ends[2 * b, :, lanes]
                scaled = state * from_start[:, lanes]
                tiled = jnp.concatenate([scaled] * (LANES // FGROUP), axis=0)
                states = jnp.where(diag, tiled, 0.0).astype(BF16)
                carried = dot_t(jnp.concatenate([states, states], axis=1), gt[h])
                cols = slice(chunk * CHUNK, (chunk + 1) * CHUNK)
                conv[rows, cols] = (y[rows, cols] + carried).astype(BF16)
            cols = slice(b * half, (b + 1) * half)
            copy = pltpu.make_async_copy(
                conv.at[rows, cols], conv_hbm.at[rows, cols], conv_sem.at[2 * b + h]
            )
            copy.start()
            conv_copies.append(copy)

    start_a = before_a * by_block[RING - 1 : RING]
    for k in range(1, RING):
        a_copies[k - 1].wait_recv()
        start_a = start_a + by_block[k - 1 : k] * a_in[k].astype(F32)
    finish(0, start_a)

    start_b = before_b * by_block[RING - 1 : RING] + over_blocks(
        2 * n_ctx - 2 - 2 * me
    ) * (start_a * by_block[1:2] + end_a)
    for k in range(1, RING):
        b_copies[k - 1].wait_recv()
        start_b = start_b + by_block[RING - 1 - k : RING - k] * b_in[k].astype(F32)
    finish(1, start_b)

    for copy in halo_copies + z_copies + a_copies + b_copies:
        copy.wait_send()
    for copy in conv_copies:
        copy.wait()


def per_device(sq, sk, sv, lq, lk, taps, res, rate):
    chans, length = sk.shape
    n_ctx = lax.axis_size("ctx")
    nz = n_ctx // RING
    groups = chans // FGROUP
    states = groups * MODES
    wide = pltpu.VMEM((chans, length), BF16)
    dma = pltpu.SemaphoreType.DMA
    scratch = [
        wide,
        wide,
        wide,
        wide,
        pltpu.VMEM(taps.shape, BF16),
        pltpu.VMEM(res.shape, F32),
        pltpu.VMEM(rate.shape, F32),
        wide,
        pltpu.VMEM((2, chans, TAPS), BF16),
        pltpu.VMEM((2, chans, TAPS), BF16),
        pltpu.VMEM((2, chans, TAPS), F32),
        pltpu.VMEM((groups, TAPS, TAPS), BF16),
        pltpu.VMEM((groups, TAPS), F32),
        pltpu.VMEM((groups, states), F32),
        pltpu.VMEM((2, CHUNK, 2 * LANES), BF16),
        pltpu.VMEM((2, CHUNK, 2 * LANES), BF16),
        pltpu.VMEM((groups, CHUNK), F32),
        wide,
        pltpu.VMEM((chans, length), F32),
        pltpu.VMEM((length // CHUNK, FGROUP, states), F32),
        pltpu.VMEM((FGROUP, states), F32),
        pltpu.VMEM((2, FGROUP, states), BF16),
        pltpu.VMEM((nz, FGROUP, states), BF16),
        pltpu.VMEM((2, FGROUP, states), BF16),
        pltpu.VMEM((RING, FGROUP, states), BF16),
        pltpu.VMEM((2, FGROUP, states), BF16),
        pltpu.VMEM((RING, FGROUP, states), BF16),
        wide,
        dma((13,)),
        dma((2,)),
        dma((2,)),
        dma((nz,)),
        dma((nz,)),
        dma((RING,)),
        dma((RING,)),
        dma((RING,)),
        dma((RING,)),
        dma((4,)),
    ]
    anywhere = pl.BlockSpec(memory_space=pl.ANY)
    conv = pl.pallas_call(
        functools.partial(kernel, n_ctx),
        out_shape=jax.ShapeDtypeStruct((chans, length), BF16),
        in_specs=[anywhere] * 7,
        out_specs=anywhere,
        scratch_shapes=scratch,
        compiler_params=pltpu.CompilerParams(
            collective_id=0, has_side_effects=True, vmem_limit_bytes=56 << 20
        ),
    )(sq, sk, sv, lk, taps, res, rate)
    return (lq.astype(F32) * conv.astype(F32)).astype(BF16)


def solution(mesh):
    in_specs = (P("chan", "ctx"),) * 5 + (P("chan", None),) * 3
    return jax.shard_map(
        per_device,
        mesh=mesh,
        in_specs=in_specs,
        out_specs=P("chan", "ctx"),
        check_vma=False,
    )
```

```python
import functools

import jax
import jax.numpy as jnp
from jax import lax
from jax.experimental import pallas as pl
from jax.experimental.pallas import tpu as pltpu
from jax.sharding import PartitionSpec as P

TAPS = 128
FGROUP = 16
MODES = 16
CHUNK = 256
RING = 8
LANES = 128
MESH = pl.DeviceIdType.MESH
F32 = jnp.float32
BF16 = jnp.bfloat16


def dot(a, b):
    return lax.dot_general(a, b, (((1,), (0,)), ((), ())), preferred_element_type=F32)


def dot_t(a, b):
    return lax.dot_general(a, b, (((1,), (1,)), ((), ())), preferred_element_type=F32)


def split_float(values):
    high = values.astype(BF16)
    low = (values - high.astype(F32)).astype(BF16)
    return high, low


def iota(shape, axis):
    return lax.broadcasted_iota(jnp.int32, shape, axis)


def kernel(
    n_ctx,
    sq_hbm,
    sk_hbm,
    sv_hbm,
    lq_hbm,
    lk_hbm,
    taps_hbm,
    modes_hbm,
    out,
    sq,
    sk,
    sv,
    lq,
    lk,
    taps,
    modes,
    mixed,
    tails,
    halo,
    first,
    gates,
    added,
    relay,
    upper_w,
    taps_f,
    pad,
    fe,
    gt,
    filt,
    x,
    y,
    ends,
    from_z,
    z_out,
    z_in,
    a_out,
    a_in,
    b_out,
    b_in,
    v_in,
    load_sem,
    halo_send,
    halo_recv,
    z_send,
    z_recv,
    a_send,
    a_recv,
    b_send,
    b_recv,
    relay_send,
    relay_recv,
    v_send,
    v_recv,
    up,
    go,
    wrap,
):
    chans, length = sk.shape
    half = length // 2
    groups = chans // FGROUP
    nz = n_ctx // RING
    me = lax.axis_index("ctx")
    plane = lax.div(me, RING)
    place = lax.rem(me, RING)
    after = lax.rem(me + 1, n_ctx)
    before = lax.rem(me + n_ctx - 1, n_ctx)

    def in_plane(k):
        return plane * RING + lax.rem(place + k, RING)

    def in_column(k):
        return lax.rem(plane + k, nz) * RING + place

    def load(n, src, dst):
        copy = pltpu.make_async_copy(src, dst, load_sem.at[n])
        copy.start()
        return copy

    tail_cols = ((half - TAPS, half), (length - TAPS, length))
    body_cols = ((0, half - TAPS), (half, length - TAPS))
    gate_cols = ((0, TAPS), (half, half + TAPS))
    rest_cols = ((TAPS, half), (half + TAPS, length))

    def load_pairs(n, pairs, columns):
        copies = []
        for lo, hi in columns:
            for src, dst in pairs:
                copies.append(load(n + len(copies), src.at[:, lo:hi], dst.at[:, lo:hi]))
        return copies

    mixed_pair = ((sk_hbm, sk), (sv_hbm, sv))
    gate_pair = ((sq_hbm, sq), (lk_hbm, lk))
    tail_loads = load_pairs(0, mixed_pair, tail_cols)
    gate_loads = load_pairs(4, gate_pair, gate_cols)
    modes_load = load(8, modes_hbm, modes)
    taps_load = load(9, taps_hbm, taps)
    body_loads = load_pairs(11, mixed_pair, body_cols)
    rest_loads = load_pairs(15, gate_pair, rest_cols)
    lq_load = load(10, lq_hbm, lq)

    hub = RING // 2 - 1
    border = nz - place
    both_true = jnp.logical_and
    negate = jnp.logical_not
    is_first = me == 0
    is_last = me == n_ctx - 1
    at_hub = place == hub
    inner_place = both_true(place >= 2, place < nz)
    at_relay = both_true(plane == 0, inner_place)
    top_edge = both_true(place == RING - 1, both_true(plane >= 1, plane < nz - 1))
    low_edge = both_true(place == 0, plane >= 2)
    edge = jnp.logical_or(top_edge, low_edge)

    barrier = pltpu.get_barrier_semaphore()

    def signal(semaphore, device):
        pl.semaphore_signal(
            semaphore, inc=1, device_id={"ctx": device}, device_id_type=MESH
        )

    pl.when(negate(jnp.logical_or(is_first, low_edge)))(lambda: signal(barrier, before))
    pl.when(negate(is_last))(lambda: signal(barrier, after))
    pl.when(negate(at_hub))(lambda: signal(barrier, plane * RING + hub))

    @pl.when(at_hub)
    def _():
        for k in range(1, RING):
            signal(barrier, in_plane(k))

    for k in range(1, nz):
        pl.when(plane + k < nz)(functools.partial(signal, barrier, in_column(k)))

    @pl.when(at_relay)
    def _():
        signal(barrier, border * RING + RING - 1)
        signal(barrier, border * RING + RING)

    greetings = (
        negate(is_first).astype(jnp.int32)
        + negate(jnp.logical_or(is_last, top_edge)).astype(jnp.int32)
        + jnp.where(at_hub, RING - 1, 1)
        + plane
        + edge.astype(jnp.int32)
    )

    for copy in tail_loads:
        copy.wait()
    for b, (lo, hi) in enumerate(tail_cols):
        product = sk[:, lo:hi] * sv[:, lo:hi]
        mixed[:, lo:hi] = product
        tails[b] = product
    pl.semaphore_wait(barrier, greetings)

    halo_copies = []
    for b, target in enumerate((after, before)):
        copy = pltpu.make_async_remote_copy(
            src_ref=tails.at[b],
            dst_ref=halo.at[b],
            send_sem=halo_send.at[b],
            recv_sem=halo_recv.at[b],
            device_id={"ctx": target},
            device_id_type=MESH,
        )
        halo_copies.append(copy)
    pl.when(negate(jnp.logical_or(is_last, top_edge)))(halo_copies[0].start)
    pl.when(negate(is_first))(halo_copies[1].start)

    pl.when(low_edge)(lambda: signal(wrap, before))
    for k in range(1, nz):
        pl.when(plane >= k)(functools.partial(signal, up.at[k], in_column(nz - k)))

    @pl.when(at_hub)
    def _():
        for k in range(1, RING):
            signal(go, in_plane(k))

    for copy in gate_loads:
        copy.wait()
    for b, (lo, hi) in enumerate(gate_cols):
        gates[b] = sq[:, lo:hi] * lk[:, lo:hi]

    def to_relay(n, source, device):
        return pltpu.make_async_remote_copy(
            src_ref=source,
            dst_ref=relay.at[n],
            send_sem=relay_send.at[n],
            recv_sem=relay_recv.at[n],
            device_id={"ctx": device},
            device_id_type=MESH,
        )

    top_device = lax.rem(nz - plane, nz)
    top_copies = [
        to_relay(0, tails.at[0], top_device),
        to_relay(1, gates.at[1], top_device),
    ]
    low_device = lax.rem(nz - plane + 1, nz)
    low_copies = [
        to_relay(2, gates.at[0], low_device),
        to_relay(3, tails.at[1], low_device),
    ]
    for copy in top_copies:
        pl.when(top_edge)(copy.start)
    for copy in low_copies:
        pl.when(low_edge)(copy.start)

    modes_load.wait()
    taps_load.wait()
    rate = modes[0:groups, :]
    res = modes[groups : 2 * groups, :]
    taps_f[...] = taps[...].astype(F32)

    def spread(values):
        pad[...] = jnp.zeros_like(pad)
        pad[:, 0:MODES] = values
        return pltpu.roll(pad[...], 0, 1, stride=MODES, stride_axis=0)

    rate_row = jnp.sum(spread(rate), axis=0, keepdims=True)
    weight = spread(res * jnp.sqrt(rate))
    weight_row = jnp.sum(weight, axis=0, keepdims=True)
    steps = iota((CHUNK, LANES), 0).astype(F32)
    for h in range(2):
        r = rate_row[:, h * LANES : (h + 1) * LANES]
        high, low = split_float(jnp.exp(-r * steps))
        gt[h, :, 0:LANES] = high
        gt[h, :, LANES:] = low
        high, low = split_float(jnp.exp(-r * (CHUNK - 1.0 - steps)))
        fe[h, :, 0:LANES] = high
        fe[h, :, LANES:] = low

    total = jnp.zeros((groups, CHUNK), F32)
    for h in range(2):
        high, low = split_float(weight[:, h * LANES : (h + 1) * LANES])
        total = total + dot_t(jnp.concatenate([high, high], axis=1), gt[h])
        total = total + dot_t(
            jnp.concatenate([low, jnp.zeros_like(low)], axis=1), gt[h]
        )
    filt[...] = total

    for copy in body_loads:
        copy.wait()
    for lo, hi in body_cols:
        mixed[:, lo:hi] = sk[:, lo:hi] * sv[:, lo:hi]
    for copy in rest_loads:
        copy.wait()

    lower_mask = iota((TAPS, TAPS), 1) >= iota((TAPS, TAPS), 0)
    blocks = length // TAPS
    firsts = (0, blocks // 2)

    def gated(rows, m, conv):
        cols = pl.ds(m * TAPS, TAPS)
        value = lk[rows, cols].astype(F32) * (sq[rows, cols].astype(F32) * conv)
        x[rows, cols] = value.astype(BF16)

    def short_group(g, _):
        rows = pl.ds(pl.multiple_of(g * FGROUP, FGROUP), FGROUP)
        line = jnp.broadcast_to(taps_f[pl.ds(g, 1), :], (TAPS, TAPS))
        skew = pltpu.roll(line, 0, 1, stride=1, stride_axis=0)
        upper = jnp.where(lower_mask, 0.0, skew).astype(BF16)
        lower = jnp.where(lower_mask, skew, 0.0).astype(BF16)
        upper_w[g] = upper
        data = []
        for m in range(blocks):
            if m in firsts:
                here = mixed[rows, m * TAPS : (m + 1) * TAPS]
                data.append(jnp.concatenate([jnp.zeros_like(here), here], axis=1))
            else:
                data.append(mixed[rows, (m - 1) * TAPS : (m + 1) * TAPS])
        short = dot(
            jnp.concatenate(data, axis=0), jnp.concatenate([upper, lower], axis=0)
        )
        for m in range(blocks):
            part = short[m * FGROUP : (m + 1) * FGROUP]
            if m in firsts:
                first[firsts.index(m), rows, :] = part
            gated(rows, m, part)
        return 0

    lax.fori_loop(0, groups, short_group, 0, unroll=4)

    diag = lax.div(iota((LANES, LANES), 0), FGROUP) == lax.div(
        iota((LANES, LANES), 1), MODES
    )

    def chunk_ends(chunk):
        for h in range(2):
            both = dot(
                x[h * LANES : (h + 1) * LANES, chunk * CHUNK : (chunk + 1) * CHUNK],
                fe[h],
            )
            own = jnp.where(diag, both[:, 0:LANES] + both[:, LANES:], 0.0)
            ends[chunk, :, h * LANES : (h + 1) * LANES] = jnp.sum(
                own.reshape(LANES // FGROUP, FGROUP, LANES), axis=0
            )

    for chunk in range(length // CHUNK):
        chunk_ends(chunk)

    chunk_decay = jnp.exp(-rate_row * float(CHUNK))
    powers = iota((RING, groups * MODES), 0).astype(F32)
    by_block = jnp.exp(-rate_row * (powers * half))
    powers = iota((nz, groups * MODES), 0).astype(F32)
    by_plane = jnp.exp(-rate_row * (powers * (half * RING)))

    def over_blocks(count):
        return jnp.exp(-rate_row * (half * count.astype(F32)))

    between = over_blocks(2 * n_ctx - 1 - 2 * me)

    def first_ends(values):
        parts = []
        for h in range(2):
            wide = dot(values[h * LANES : (h + 1) * LANES, :], fe[h, 0:TAPS, :])
            own = jnp.where(diag, wide[:, 0:LANES] + wide[:, LANES:], 0.0)
            parts.append(
                jnp.sum(own.reshape(LANES // FGROUP, FGROUP, LANES), axis=0)
            )
        return jnp.concatenate(parts, axis=1)

    def send(source, target, k, send_sem, recv_sem, device):
        return pltpu.make_async_remote_copy(
            src_ref=source,
            dst_ref=target.at[k],
            send_sem=send_sem.at[k],
            recv_sem=recv_sem.at[k],
            device_id={"ctx": device},
            device_id_type=MESH,
        )

    z_copies = []
    is_down = []
    is_early = []
    for k in range(1, nz):
        down = plane + k >= nz
        early = both_true(edge, down)
        if k == nz - 1:
            early = both_true(early, negate(low_edge))
        kind = jnp.where(down, jnp.where(early, 2, 1), 0)
        z_copies.append(send(z_out.at[kind], z_in, k, z_send, z_recv, in_column(k)))
        is_down.append(down)
        is_early.append(early)

    def block_ends():
        end_a = ends[0] * chunk_decay + ends[1]
        end_b = ends[2] * chunk_decay + ends[3]
        return end_a, end_b + end_a * between

    @pl.when(is_first)
    def _():
        halo[0] = jnp.zeros_like(halo[0])

    @pl.when(is_last)
    def _():
        halo[1] = tails[0]

    def add_halo(b):
        away = jnp.logical_or(both_true(b == 0, is_first), both_true(b == 1, is_last))
        copy = pltpu.make_async_remote_copy(
            src_ref=tails.at[b],
            dst_ref=halo.at[b],
            send_sem=halo_send.at[b],
            recv_sem=halo_recv.at[b],
            device_id={"ctx": after},
            device_id_type=MESH,
        )
        pl.when(negate(away))(copy.wait_recv)
        cols = pl.ds(pl.multiple_of(b * half, TAPS), TAPS)

        def group(g, _):
            rows = pl.ds(pl.multiple_of(g * FGROUP, FGROUP), FGROUP)
            extra = dot(halo[b, rows, :], upper_w[g])
            query = sq[rows, cols].astype(F32)
            key = lk[rows, cols].astype(F32)
            added[0, rows, :] = (key * (query * extra)).astype(BF16)
            x[rows, cols] = (key * (query * (extra + first[b, rows, :]))).astype(BF16)
            return 0

        lax.fori_loop(0, groups, group, 0, unroll=8)
        ends[2 * b] += first_ends(added[0])

    near = jnp.where(place == 0, 1, 0)
    add_halo(near)

    @pl.when(edge)
    def _():
        z_out[2] = block_ends()[1].astype(BF16)
        for k in range(1, nz):
            pl.when(is_early[k - 1])(z_copies[k - 1].start)

    @pl.when(top_edge)
    def _():
        pl.semaphore_wait(wrap, 1)
        halo_copies[0].start()

    add_halo(1 - near)
    end_a, both = block_ends()
    z_out[0] = end_a.astype(BF16)
    z_out[1] = both.astype(BF16)
    for k in range(1, nz):
        late = both_true(is_down[k - 1], negate(is_early[k - 1]))
        pl.when(late)(z_copies[k - 1].start)
    for k in range(1, nz):

        @pl.when(negate(is_down[k - 1]))
        def _():
            pl.semaphore_wait(up.at[k], 1)
            z_copies[k - 1].start()

    def inner_group(g, _):
        rows = pl.ds(pl.multiple_of(g * FGROUP, FGROUP), FGROUP)
        line = jnp.broadcast_to(filt[pl.ds(g, 1), :], (TAPS, CHUNK))
        skew = pltpu.roll(line, 0, 1, stride=1, stride_axis=0)
        near = jnp.where(lower_mask, skew[:, 0:TAPS], 0.0).astype(BF16)
        far = skew[:, TAPS:].astype(BF16)
        table = jnp.concatenate(
            [
                jnp.concatenate([near, far], axis=1),
                jnp.concatenate([jnp.zeros_like(near), near], axis=1),
            ],
            axis=0,
        )
        chunks = length // CHUNK
        data = [x[rows, c * CHUNK : (c + 1) * CHUNK] for c in range(chunks)]
        inner = dot(jnp.concatenate(data, axis=0), table)
        for c in range(chunks):
            y[rows, c * CHUNK : (c + 1) * CHUNK] = inner[
                c * FGROUP : (c + 1) * FGROUP
            ]
        return 0

    lax.fori_loop(0, 6, inner_group, 0, unroll=3)

    def from_planes(first_half):
        from_z[...] = jnp.zeros_like(from_z)
        for k in range(1, nz):
            power = k - 1 if first_half else nz - 1 - k

            @pl.when((plane >= k) if first_half else (plane < k))
            def _():
                z_copies[k - 1].wait_recv()
                from_z[...] += by_plane[power : power + 1] * z_in[k].astype(F32)

        if not first_half:

            @pl.when(both_true(inner_place, plane < border))
            def _():
                pl.when(plane >= 1)(v_copies[0].wait_recv)
                count = jnp.maximum(RING * (border - plane) - 1 - place, 0)
                from_z[...] += over_blocks(count) * v_in[...].astype(F32)

        return from_z[...]

    one_plane = by_plane[1:2]
    before_a = from_planes(True)
    a_out[0] = (before_a * one_plane + end_a).astype(BF16)
    a_out[1] = before_a.astype(BF16)
    a_copies = [
        send(a_out.at[lax.div(place + k, RING)], a_in, k, a_send, a_recv, in_plane(k))
        for k in range(1, RING)
    ]
    pl.when(negate(at_hub))(lambda: pl.semaphore_wait(go, 1))
    for copy in a_copies:
        copy.start()

    v_copies = [
        pltpu.make_async_remote_copy(
            src_ref=v_in,
            dst_ref=v_in,
            send_sem=v_send.at[k],
            recv_sem=v_recv,
            device_id={"ctx": in_column(k)},
            device_id_type=MESH,
        )
        for k in range(1, nz - 1)
    ]

    @pl.when(at_relay)
    def _():
        for n in range(4):
            to_relay(n, relay.at[n], top_device).wait_recv()

        def group(g, _):
            rows = pl.ds(pl.multiple_of(g * FGROUP, FGROUP), FGROUP)
            ended = jnp.concatenate([relay[0, rows, :], relay[3, rows, :]], axis=0)
            extra = dot(ended, upper_w[g])
            for b in range(2):
                part = extra[b * FGROUP : (b + 1) * FGROUP]
                gate = relay[2 - b, rows, :].astype(F32)
                added[b, rows, :] = (gate * part).astype(BF16)
            return 0

        lax.fori_loop(0, groups, group, 0, unroll=8)
        far = over_blocks(2 * RING * (place - 1))
        state = first_ends(added[1]) + first_ends(added[0]) * far
        v_in[...] = (state * chunk_decay).astype(BF16)
        for k in range(1, nz - 1):
            pl.when(k < border)(v_copies[k - 1].start)

    before_b = from_planes(False)
    b_out[0] = before_b.astype(BF16)
    b_out[1] = (before_b * one_plane + both).astype(BF16)
    b_copies = [
        send(b_out.at[lax.div(place + k, RING)], b_in, k, b_send, b_recv, in_plane(k))
        for k in range(1, RING)
    ]
    for copy in b_copies:
        copy.start()

    lax.fori_loop(6, groups, inner_group, 0, unroll=5)

    from_start = weight_row * jnp.exp(-rate_row)
    lq_load.wait()

    def finish(b, start):
        for h in range(2):
            lanes = slice(h * LANES, (h + 1) * LANES)
            rows = slice(h * LANES, (h + 1) * LANES)
            state = start[:, lanes]
            for c in range(2):
                chunk = 2 * b + c
                if c == 1:
                    state = state * chunk_decay[:, lanes] + ends[2 * b, :, lanes]
                scaled = state * from_start[:, lanes]
                tiled = jnp.concatenate([scaled] * (LANES // FGROUP), axis=0)
                states = jnp.where(diag, tiled, 0.0).astype(BF16)
                carried = dot_t(jnp.concatenate([states, states], axis=1), gt[h])
                cols = slice(chunk * CHUNK, (chunk + 1) * CHUNK)
                value = lq[rows, cols].astype(F32) * (y[rows, cols] + carried)
                out[rows, cols] = value.astype(BF16)

    start_a = before_a * by_block[RING - 1 : RING]
    for k in range(1, RING):
        a_copies[k - 1].wait_recv()
        start_a = start_a + by_block[k - 1 : k] * a_in[k].astype(F32)
    finish(0, start_a)

    start_b = before_b * by_block[RING - 1 : RING] + over_blocks(
        2 * n_ctx - 2 - 2 * me
    ) * (start_a * by_block[1:2] + end_a)
    for k in range(1, RING):
        b_copies[k - 1].wait_recv()
        start_b = start_b + by_block[RING - 1 - k : RING - k] * b_in[k].astype(F32)
    finish(1, start_b)

    pl.when(negate(is_last))(halo_copies[0].wait_send)
    pl.when(negate(is_first))(halo_copies[1].wait_send)
    for copy in top_copies:
        pl.when(top_edge)(copy.wait_send)
    for copy in low_copies:
        pl.when(low_edge)(copy.wait_send)
    for k in range(1, nz - 1):
        pl.when(both_true(at_relay, k < border))(v_copies[k - 1].wait_send)
    for copy in z_copies + a_copies + b_copies:
        copy.wait_send()


def per_device(sq, sk, sv, lq, lk, taps, res, rate):
    chans, length = sk.shape
    n_ctx = lax.axis_size("ctx")
    nz = n_ctx // RING
    groups = chans // FGROUP
    states = groups * MODES
    wide = pltpu.VMEM((chans, length), BF16)
    dma = pltpu.SemaphoreType.DMA
    scratch = [
        wide,
        wide,
        wide,
        wide,
        wide,
        pltpu.VMEM(taps.shape, BF16),
        pltpu.VMEM((2 * groups, MODES), F32),
        wide,
        pltpu.VMEM((2, chans, TAPS), BF16),
        pltpu.VMEM((2, chans, TAPS), BF16),
        pltpu.VMEM((2, chans, TAPS), F32),
        pltpu.VMEM((2, chans, TAPS), BF16),
        pltpu.VMEM((2, chans, TAPS), BF16),
        pltpu.VMEM((4, chans, TAPS), BF16),
        pltpu.VMEM((groups, TAPS, TAPS), BF16),
        pltpu.VMEM((groups, TAPS), F32),
        pltpu.VMEM((groups, states), F32),
        pltpu.VMEM((2, CHUNK, 2 * LANES), BF16),
        pltpu.VMEM((2, CHUNK, 2 * LANES), BF16),
        pltpu.VMEM((groups, CHUNK), F32),
        wide,
        pltpu.VMEM((chans, length), F32),
        pltpu.VMEM((length // CHUNK, FGROUP, states), F32),
        pltpu.VMEM((FGROUP, states), F32),
        pltpu.VMEM((3, FGROUP, states), BF16),
        pltpu.VMEM((nz, FGROUP, states), BF16),
        pltpu.VMEM((2, FGROUP, states), BF16),
        pltpu.VMEM((RING, FGROUP, states), BF16),
        pltpu.VMEM((2, FGROUP, states), BF16),
        pltpu.VMEM((RING, FGROUP, states), BF16),
        pltpu.VMEM((FGROUP, states), BF16),
        dma((19,)),
        dma((2,)),
        dma((2,)),
        dma((nz,)),
        dma((nz,)),
        dma((RING,)),
        dma((RING,)),
        dma((RING,)),
        dma((RING,)),
        dma((4,)),
        dma((4,)),
        dma((nz,)),
        dma(()),
        pltpu.SemaphoreType.REGULAR((nz,)),
        pltpu.SemaphoreType.REGULAR,
        pltpu.SemaphoreType.REGULAR,
    ]
    anywhere = pl.BlockSpec(memory_space=pl.ANY)
    modes = jnp.concatenate([rate, res], axis=0)
    return pl.pallas_call(
        functools.partial(kernel, n_ctx),
        out_shape=jax.ShapeDtypeStruct((chans, length), BF16),
        in_specs=[anywhere] * 7,
        out_specs=pl.BlockSpec(memory_space=pltpu.VMEM),
        scratch_shapes=scratch,
        compiler_params=pltpu.CompilerParams(
            collective_id=0, has_side_effects=True, vmem_limit_bytes=53 << 20
        ),
    )(sq, sk, sv, lq, lk, taps, modes)


def solution(mesh):
    in_specs = (P("chan", "ctx"),) * 5 + (P("chan", None),) * 3
    return jax.shard_map(
        per_device,
        mesh=mesh,
        in_specs=in_specs,
        out_specs=P("chan", "ctx"),
        check_vma=False,
    )
```

```python
import functools

import jax
import jax.numpy as jnp
from jax import lax
from jax.experimental import pallas as pl
from jax.experimental.pallas import tpu as pltpu
from jax.sharding import PartitionSpec as P

TAPS = 128
FGROUP = 16
MODES = 16
CHUNK = 256
RING = 8
LANES = 128
MESH = pl.DeviceIdType.MESH
F32 = jnp.float32
BF16 = jnp.bfloat16


def dot(a, b):
    return lax.dot_general(a, b, (((1,), (0,)), ((), ())), preferred_element_type=F32)


def dot_t(a, b):
    return lax.dot_general(a, b, (((1,), (1,)), ((), ())), preferred_element_type=F32)


def split_float(values):
    high = values.astype(BF16)
    low = (values - high.astype(F32)).astype(BF16)
    return high, low


def iota(shape, axis):
    return lax.broadcasted_iota(jnp.int32, shape, axis)


def kernel(
    n_ctx,
    sq_hbm,
    sk_hbm,
    sv_hbm,
    lq_hbm,
    lk_hbm,
    taps_hbm,
    modes_hbm,
    out,
    sq,
    sk,
    sv,
    lq,
    lk,
    taps,
    modes,
    mixed,
    tails,
    halo,
    first,
    gates,
    added,
    relay,
    upper_w,
    taps_f,
    pad,
    fe,
    gt,
    filt,
    x,
    y,
    ends,
    from_z,
    z_out,
    z_in,
    a_out,
    a_in,
    b_out,
    b_in,
    v_in,
    load_sem,
    halo_send,
    halo_recv,
    z_send,
    z_recv,
    a_send,
    a_recv,
    b_send,
    b_recv,
    relay_send,
    relay_recv,
    v_send,
    v_recv,
    up,
    go,
    wrap,
):
    chans, length = sk.shape
    half = length // 2
    groups = chans // FGROUP
    nz = n_ctx // RING
    me = lax.axis_index("ctx")
    plane = lax.div(me, RING)
    place = lax.rem(me, RING)
    after = lax.rem(me + 1, n_ctx)
    before = lax.rem(me + n_ctx - 1, n_ctx)

    def in_plane(k):
        return plane * RING + lax.rem(place + k, RING)

    def in_column(k):
        return lax.rem(plane + k, nz) * RING + place

    def load(n, src, dst):
        copy = pltpu.make_async_copy(src, dst, load_sem.at[n])
        copy.start()
        return copy

    tail_cols = ((half - TAPS, half), (length - TAPS, length))
    body_cols = ((0, half - TAPS), (half, length - TAPS))
    gate_cols = ((0, TAPS), (half, half + TAPS))
    rest_cols = ((TAPS, half), (half + TAPS, length))

    def load_pairs(n, pairs, columns):
        copies = []
        for lo, hi in columns:
            for src, dst in pairs:
                copies.append(load(n + len(copies), src.at[:, lo:hi], dst.at[:, lo:hi]))
        return copies

    mixed_pair = ((sk_hbm, sk), (sv_hbm, sv))
    gate_pair = ((sq_hbm, sq), (lk_hbm, lk))
    tail_loads = load_pairs(0, mixed_pair, tail_cols)
    gate_loads = load_pairs(4, gate_pair, gate_cols)
    modes_load = load(8, modes_hbm, modes)
    taps_load = load(9, taps_hbm, taps)
    body_loads = load_pairs(11, mixed_pair, body_cols)
    rest_loads = load_pairs(15, gate_pair, rest_cols)
    lq_load = load(10, lq_hbm, lq)

    hub = RING // 2 - 1
    border = nz - place
    both_true = jnp.logical_and
    negate = jnp.logical_not
    is_first = me == 0
    is_last = me == n_ctx - 1
    at_hub = place == hub
    inner_place = both_true(place >= 2, place < nz)
    at_relay = both_true(plane == 0, inner_place)
    top_edge = both_true(place == RING - 1, both_true(plane >= 1, plane < nz - 1))
    low_edge = both_true(place == 0, plane >= 2)
    edge = jnp.logical_or(top_edge, low_edge)

    is_late_column = both_true(lax.axis_index("chan") == 0, place == 0)
    is_late = both_true(is_late_column, plane == 0)
    is_known = []
    for k in range(1, nz):
        other = lax.rem(plane + k, nz)
        other_late = both_true(is_late_column, other == 0)
        known = jnp.logical_or(both_true(other < plane, negate(other_late)), is_late)
        is_known.append(known)
    entered = sum(known.astype(jnp.int32) for known in is_known)

    barrier = pltpu.get_barrier_semaphore()

    def signal(semaphore, device):
        pl.semaphore_signal(
            semaphore, inc=1, device_id={"ctx": device}, device_id_type=MESH
        )

    pl.when(negate(jnp.logical_or(is_first, low_edge)))(lambda: signal(barrier, before))
    pl.when(negate(is_last))(lambda: signal(barrier, after))
    pl.when(negate(at_hub))(lambda: signal(barrier, plane * RING + hub))

    for k in range(1, nz):
        pl.when(negate(is_known[k - 1]))(
            functools.partial(signal, barrier, in_column(k))
        )

    @pl.when(at_relay)
    def _():
        signal(barrier, border * RING + RING - 1)
        signal(barrier, border * RING + RING)

    greetings = (
        negate(is_first).astype(jnp.int32)
        + negate(jnp.logical_or(is_last, top_edge)).astype(jnp.int32)
        + jnp.where(at_hub, RING - 1, 0)
        + entered
        + edge.astype(jnp.int32)
    )

    for copy in tail_loads:
        copy.wait()
    for b, (lo, hi) in enumerate(tail_cols):
        product = sk[:, lo:hi] * sv[:, lo:hi]
        mixed[:, lo:hi] = product
        tails[b] = product
    pl.semaphore_wait(barrier, greetings)

    halo_copies = []
    for b, target in enumerate((after, before)):
        copy = pltpu.make_async_remote_copy(
            src_ref=tails.at[b],
            dst_ref=halo.at[b],
            send_sem=halo_send.at[b],
            recv_sem=halo_recv.at[b],
            device_id={"ctx": target},
            device_id_type=MESH,
        )
        halo_copies.append(copy)
    pl.when(negate(jnp.logical_or(is_last, top_edge)))(halo_copies[0].start)
    pl.when(negate(is_first))(halo_copies[1].start)

    pl.when(low_edge)(lambda: signal(wrap, before))
    for k in range(1, nz):
        pl.when(is_known[nz - k - 1])(
            functools.partial(signal, up.at[k], in_column(nz - k))
        )

    @pl.when(at_hub)
    def _():
        for k in range(1, RING):
            signal(go, in_plane(k))

    for copy in gate_loads:
        copy.wait()
    for b, (lo, hi) in enumerate(gate_cols):
        gates[b] = sq[:, lo:hi] * lk[:, lo:hi]

    def to_relay(n, source, device):
        return pltpu.make_async_remote_copy(
            src_ref=source,
            dst_ref=relay.at[n],
            send_sem=relay_send.at[n],
            recv_sem=relay_recv.at[n],
            device_id={"ctx": device},
            device_id_type=MESH,
        )

    top_device = lax.rem(nz - plane, nz)
    top_copies = [
        to_relay(0, tails.at[0], top_device),
        to_relay(1, gates.at[1], top_device),
    ]
    low_device = lax.rem(nz - plane + 1, nz)
    low_copies = [
        to_relay(2, gates.at[0], low_device),
        to_relay(3, tails.at[1], low_device),
    ]
    for copy in top_copies:
        pl.when(top_edge)(copy.start)
    for copy in low_copies:
        pl.when(low_edge)(copy.start)

    modes_load.wait()
    taps_load.wait()
    rate = modes[0:groups, :]
    res = modes[groups : 2 * groups, :]
    taps_f[...] = taps[...].astype(F32)

    def spread(values):
        pad[...] = jnp.zeros_like(pad)
        pad[:, 0:MODES] = values
        return pltpu.roll(pad[...], 0, 1, stride=MODES, stride_axis=0)

    rate_row = jnp.sum(spread(rate), axis=0, keepdims=True)
    weight = spread(res * jnp.sqrt(rate))
    weight_row = jnp.sum(weight, axis=0, keepdims=True)
    steps = iota((CHUNK, LANES), 0).astype(F32)
    for h in range(2):
        r = rate_row[:, h * LANES : (h + 1) * LANES]
        high, low = split_float(jnp.exp(-r * steps))
        gt[h, :, 0:LANES] = high
        gt[h, :, LANES:] = low
        high, low = split_float(jnp.exp(-r * (CHUNK - 1.0 - steps)))
        fe[h, :, 0:LANES] = high
        fe[h, :, LANES:] = low

    total = jnp.zeros((groups, CHUNK), F32)
    for h in range(2):
        high, low = split_float(weight[:, h * LANES : (h + 1) * LANES])
        total = total + dot_t(jnp.concatenate([high, high], axis=1), gt[h])
        total = total + dot_t(
            jnp.concatenate([low, jnp.zeros_like(low)], axis=1), gt[h]
        )
    filt[...] = total

    for copy in body_loads:
        copy.wait()
    for lo, hi in body_cols:
        mixed[:, lo:hi] = sk[:, lo:hi] * sv[:, lo:hi]
    for copy in rest_loads:
        copy.wait()

    lower_mask = iota((TAPS, TAPS), 1) >= iota((TAPS, TAPS), 0)
    blocks = length // TAPS
    firsts = (0, blocks // 2)

    def gated(rows, m, conv):
        cols = pl.ds(m * TAPS, TAPS)
        value = lk[rows, cols].astype(F32) * (sq[rows, cols].astype(F32) * conv)
        x[rows, cols] = value.astype(BF16)

    def short_group(g, _):
        rows = pl.ds(pl.multiple_of(g * FGROUP, FGROUP), FGROUP)
        line = jnp.broadcast_to(taps_f[pl.ds(g, 1), :], (TAPS, TAPS))
        skew = pltpu.roll(line, 0, 1, stride=1, stride_axis=0)
        upper = jnp.where(lower_mask, 0.0, skew).astype(BF16)
        lower = jnp.where(lower_mask, skew, 0.0).astype(BF16)
        upper_w[g] = upper
        data = []
        for m in range(blocks):
            if m in firsts:
                here = mixed[rows, m * TAPS : (m + 1) * TAPS]
                data.append(jnp.concatenate([jnp.zeros_like(here), here], axis=1))
            else:
                data.append(mixed[rows, (m - 1) * TAPS : (m + 1) * TAPS])
        short = dot(
            jnp.concatenate(data, axis=0), jnp.concatenate([upper, lower], axis=0)
        )
        for m in range(blocks):
            part = short[m * FGROUP : (m + 1) * FGROUP]
            if m in firsts:
                first[firsts.index(m), rows, :] = part
            gated(rows, m, part)
        return 0

    lax.fori_loop(0, groups, short_group, 0, unroll=4)

    diag = lax.div(iota((LANES, LANES), 0), FGROUP) == lax.div(
        iota((LANES, LANES), 1), MODES
    )

    def chunk_ends(chunk):
        for h in range(2):
            both = dot(
                x[h * LANES : (h + 1) * LANES, chunk * CHUNK : (chunk + 1) * CHUNK],
                fe[h],
            )
            own = jnp.where(diag, both[:, 0:LANES] + both[:, LANES:], 0.0)
            ends[chunk, :, h * LANES : (h + 1) * LANES] = jnp.sum(
                own.reshape(LANES // FGROUP, FGROUP, LANES), axis=0
            )

    for chunk in range(length // CHUNK):
        chunk_ends(chunk)

    chunk_decay = jnp.exp(-rate_row * float(CHUNK))
    powers = iota((RING, groups * MODES), 0).astype(F32)
    by_block = jnp.exp(-rate_row * (powers * half))
    powers = iota((nz, groups * MODES), 0).astype(F32)
    by_plane = jnp.exp(-rate_row * (powers * (half * RING)))

    def over_blocks(count):
        return jnp.exp(-rate_row * (half * count.astype(F32)))

    between = over_blocks(2 * n_ctx - 1 - 2 * me)

    def first_ends(values):
        parts = []
        for h in range(2):
            wide = dot(values[h * LANES : (h + 1) * LANES, :], fe[h, 0:TAPS, :])
            own = jnp.where(diag, wide[:, 0:LANES] + wide[:, LANES:], 0.0)
            parts.append(
                jnp.sum(own.reshape(LANES // FGROUP, FGROUP, LANES), axis=0)
            )
        return jnp.concatenate(parts, axis=1)

    def send(source, target, k, send_sem, recv_sem, device):
        return pltpu.make_async_remote_copy(
            src_ref=source,
            dst_ref=target.at[k],
            send_sem=send_sem.at[k],
            recv_sem=recv_sem.at[k],
            device_id={"ctx": device},
            device_id_type=MESH,
        )

    z_copies = []
    is_down = []
    is_early = []
    for k in range(1, nz):
        down = plane + k >= nz
        early = both_true(edge, down)
        if k == nz - 1:
            early = both_true(early, negate(low_edge))
        kind = jnp.where(down, jnp.where(early, 2, 1), 0)
        z_copies.append(send(z_out.at[kind], z_in, k, z_send, z_recv, in_column(k)))
        is_down.append(down)
        is_early.append(early)

    def block_ends():
        end_a = ends[0] * chunk_decay + ends[1]
        end_b = ends[2] * chunk_decay + ends[3]
        return end_a, end_b + end_a * between

    @pl.when(is_first)
    def _():
        halo[0] = jnp.zeros_like(halo[0])

    @pl.when(is_last)
    def _():
        halo[1] = tails[0]

    def add_halo(b):
        away = jnp.logical_or(both_true(b == 0, is_first), both_true(b == 1, is_last))
        copy = pltpu.make_async_remote_copy(
            src_ref=tails.at[b],
            dst_ref=halo.at[b],
            send_sem=halo_send.at[b],
            recv_sem=halo_recv.at[b],
            device_id={"ctx": after},
            device_id_type=MESH,
        )
        pl.when(negate(away))(copy.wait_recv)
        cols = pl.ds(pl.multiple_of(b * half, TAPS), TAPS)

        def group(g, _):
            rows = pl.ds(pl.multiple_of(g * FGROUP, FGROUP), FGROUP)
            extra = dot(halo[b, rows, :], upper_w[g])
            query = sq[rows, cols].astype(F32)
            key = lk[rows, cols].astype(F32)
            added[0, rows, :] = (key * (query * extra)).astype(BF16)
            x[rows, cols] = (key * (query * (extra + first[b, rows, :]))).astype(BF16)
            return 0

        lax.fori_loop(0, groups, group, 0, unroll=16)
        ends[2 * b] += first_ends(added[0])

    near = 1 - lax.rem(place, 2)
    add_halo(near)

    def start_column(k, wanted):
        @pl.when(wanted)
        def _():
            pl.when(negate(is_known[k - 1]))(lambda: pl.semaphore_wait(up.at[k], 1))
            z_copies[k - 1].start()

    @pl.when(edge)
    def _():
        z_out[2] = block_ends()[1].astype(BF16)
        for k in range(1, nz):
            start_column(k, both_true(is_early[k - 1], is_known[k - 1]))
        for k in range(1, nz):
            start_column(k, both_true(is_early[k - 1], negate(is_known[k - 1])))

    @pl.when(top_edge)
    def _():
        pl.semaphore_wait(wrap, 1)
        halo_copies[0].start()

    add_halo(1 - near)
    end_a, both = block_ends()
    z_out[0] = end_a.astype(BF16)
    z_out[1] = both.astype(BF16)
    for k in range(1, nz):
        late = both_true(is_down[k - 1], negate(is_early[k - 1]))
        start_column(k, late)
    for k in range(1, nz):
        start_column(k, negate(is_down[k - 1]))

    def inner_group(g, _):
        rows = pl.ds(pl.multiple_of(g * FGROUP, FGROUP), FGROUP)
        line = jnp.broadcast_to(filt[pl.ds(g, 1), :], (TAPS, CHUNK))
        skew = pltpu.roll(line, 0, 1, stride=1, stride_axis=0)
        near = jnp.where(lower_mask, skew[:, 0:TAPS], 0.0).astype(BF16)
        far = skew[:, TAPS:].astype(BF16)
        table = jnp.concatenate(
            [
                jnp.concatenate([near, far], axis=1),
                jnp.concatenate([jnp.zeros_like(near), near], axis=1),
            ],
            axis=0,
        )
        chunks = length // CHUNK
        data = [x[rows, c * CHUNK : (c + 1) * CHUNK] for c in range(chunks)]
        inner = dot(jnp.concatenate(data, axis=0), table)
        for c in range(chunks):
            y[rows, c * CHUNK : (c + 1) * CHUNK] = inner[
                c * FGROUP : (c + 1) * FGROUP
            ]
        return 0

    lax.fori_loop(0, 6, inner_group, 0, unroll=3)

    def from_planes(first_half):
        from_z[...] = jnp.zeros_like(from_z)
        for k in range(1, nz):
            power = k - 1 if first_half else nz - 1 - k

            @pl.when((plane >= k) if first_half else (plane < k))
            def _():
                z_copies[k - 1].wait_recv()
                from_z[...] += by_plane[power : power + 1] * z_in[k].astype(F32)

        if not first_half:

            @pl.when(both_true(inner_place, plane < border))
            def _():
                pl.when(plane >= 1)(v_copies[0].wait_recv)
                count = jnp.maximum(RING * (border - plane) - 1 - place, 0)
                from_z[...] += over_blocks(count) * v_in[...].astype(F32)

        return from_z[...]

    one_plane = by_plane[1:2]
    before_a = from_planes(True)
    a_out[0] = (before_a * one_plane + end_a).astype(BF16)
    a_out[1] = before_a.astype(BF16)
    a_copies = [
        send(a_out.at[lax.div(place + k, RING)], a_in, k, a_send, a_recv, in_plane(k))
        for k in range(1, RING)
    ]
    pl.when(negate(at_hub))(lambda: pl.semaphore_wait(go, 1))
    for copy in a_copies:
        copy.start()

    v_copies = [
        pltpu.make_async_remote_copy(
            src_ref=v_in,
            dst_ref=v_in,
            send_sem=v_send.at[k],
            recv_sem=v_recv,
            device_id={"ctx": in_column(k)},
            device_id_type=MESH,
        )
        for k in range(1, nz - 1)
    ]

    @pl.when(at_relay)
    def _():
        for n in range(4):
            to_relay(n, relay.at[n], top_device).wait_recv()

        def group(g, _):
            rows = pl.ds(pl.multiple_of(g * FGROUP, FGROUP), FGROUP)
            ended = jnp.concatenate([relay[0, rows, :], relay[3, rows, :]], axis=0)
            extra = dot(ended, upper_w[g])
            for b in range(2):
                part = extra[b * FGROUP : (b + 1) * FGROUP]
                gate = relay[2 - b, rows, :].astype(F32)
                added[b, rows, :] = (gate * part).astype(BF16)
            return 0

        lax.fori_loop(0, groups, group, 0, unroll=16)
        far = over_blocks(2 * RING * (place - 1))
        state = first_ends(added[1]) + first_ends(added[0]) * far
        v_in[...] = (state * chunk_decay).astype(BF16)
        for k in range(1, nz - 1):
            pl.when(k < border)(v_copies[k - 1].start)

    before_b = from_planes(False)
    b_out[0] = before_b.astype(BF16)
    b_out[1] = (before_b * one_plane + both).astype(BF16)
    b_copies = [
        send(b_out.at[lax.div(place + k, RING)], b_in, k, b_send, b_recv, in_plane(k))
        for k in range(1, RING)
    ]
    for copy in b_copies:
        copy.start()

    lax.fori_loop(6, groups, inner_group, 0, unroll=5)

    from_start = weight_row * jnp.exp(-rate_row)
    lq_load.wait()

    def finish(b, start):
        for h in range(2):
            lanes = slice(h * LANES, (h + 1) * LANES)
            rows = slice(h * LANES, (h + 1) * LANES)
            state = start[:, lanes]
            for c in range(2):
                chunk = 2 * b + c
                if c == 1:
                    state = state * chunk_decay[:, lanes] + ends[2 * b, :, lanes]
                scaled = state * from_start[:, lanes]
                tiled = jnp.concatenate([scaled] * (LANES // FGROUP), axis=0)
                states = jnp.where(diag, tiled, 0.0).astype(BF16)
                carried = dot_t(jnp.concatenate([states, states], axis=1), gt[h])
                cols = slice(chunk * CHUNK, (chunk + 1) * CHUNK)
                value = lq[rows, cols].astype(F32) * (y[rows, cols] + carried)
                out[rows, cols] = value.astype(BF16)

    start_a = before_a * by_block[RING - 1 : RING]
    for k in range(1, RING):
        a_copies[k - 1].wait_recv()
        start_a = start_a + by_block[k - 1 : k] * a_in[k].astype(F32)
    finish(0, start_a)

    start_b = before_b * by_block[RING - 1 : RING] + over_blocks(
        2 * n_ctx - 2 - 2 * me
    ) * (start_a * by_block[1:2] + end_a)
    for k in range(1, RING):
        b_copies[k - 1].wait_recv()
        start_b = start_b + by_block[RING - 1 - k : RING - k] * b_in[k].astype(F32)
    finish(1, start_b)

    pl.when(negate(is_last))(halo_copies[0].wait_send)
    pl.when(negate(is_first))(halo_copies[1].wait_send)
    for copy in top_copies:
        pl.when(top_edge)(copy.wait_send)
    for copy in low_copies:
        pl.when(low_edge)(copy.wait_send)
    for k in range(1, nz - 1):
        pl.when(both_true(at_relay, k < border))(v_copies[k - 1].wait_send)
    for copy in z_copies + a_copies + b_copies:
        copy.wait_send()


def per_device(sq, sk, sv, lq, lk, taps, res, rate):
    chans, length = sk.shape
    n_ctx = lax.axis_size("ctx")
    nz = n_ctx // RING
    groups = chans // FGROUP
    states = groups * MODES
    wide = pltpu.VMEM((chans, length), BF16)
    dma = pltpu.SemaphoreType.DMA
    scratch = [
        wide,
        wide,
        wide,
        wide,
        wide,
        pltpu.VMEM(taps.shape, BF16),
        pltpu.VMEM((2 * groups, MODES), F32),
        wide,
        pltpu.VMEM((2, chans, TAPS), BF16),
        pltpu.VMEM((2, chans, TAPS), BF16),
        pltpu.VMEM((2, chans, TAPS), F32),
        pltpu.VMEM((2, chans, TAPS), BF16),
        pltpu.VMEM((2, chans, TAPS), BF16),
        pltpu.VMEM((4, chans, TAPS), BF16),
        pltpu.VMEM((groups, TAPS, TAPS), BF16),
        pltpu.VMEM((groups, TAPS), F32),
        pltpu.VMEM((groups, states), F32),
        pltpu.VMEM((2, CHUNK, 2 * LANES), BF16),
        pltpu.VMEM((2, CHUNK, 2 * LANES), BF16),
        pltpu.VMEM((groups, CHUNK), F32),
        wide,
        pltpu.VMEM((chans, length), F32),
        pltpu.VMEM((length // CHUNK, FGROUP, states), F32),
        pltpu.VMEM((FGROUP, states), F32),
        pltpu.VMEM((3, FGROUP, states), BF16),
        pltpu.VMEM((nz, FGROUP, states), BF16),
        pltpu.VMEM((2, FGROUP, states), BF16),
        pltpu.VMEM((RING, FGROUP, states), BF16),
        pltpu.VMEM((2, FGROUP, states), BF16),
        pltpu.VMEM((RING, FGROUP, states), BF16),
        pltpu.VMEM((FGROUP, states), BF16),
        dma((19,)),
        dma((2,)),
        dma((2,)),
        dma((nz,)),
        dma((nz,)),
        dma((RING,)),
        dma((RING,)),
        dma((RING,)),
        dma((RING,)),
        dma((4,)),
        dma((4,)),
        dma((nz,)),
        dma(()),
        pltpu.SemaphoreType.REGULAR((nz,)),
        pltpu.SemaphoreType.REGULAR,
        pltpu.SemaphoreType.REGULAR,
    ]
    anywhere = pl.BlockSpec(memory_space=pl.ANY)
    modes = jnp.concatenate([rate, res], axis=0)
    return pl.pallas_call(
        functools.partial(kernel, n_ctx),
        out_shape=jax.ShapeDtypeStruct((chans, length), BF16),
        in_specs=[anywhere] * 7,
        out_specs=pl.BlockSpec(memory_space=pltpu.VMEM),
        scratch_shapes=scratch,
        compiler_params=pltpu.CompilerParams(
            collective_id=0, has_side_effects=True, vmem_limit_bytes=53 << 20
        ),
    )(sq, sk, sv, lq, lk, taps, modes)


def solution(mesh):
    in_specs = (P("chan", "ctx"),) * 5 + (P("chan", None),) * 3
    return jax.shard_map(
        per_device,
        mesh=mesh,
        in_specs=in_specs,
        out_specs=P("chan", "ctx"),
        check_vma=False,
    )
```

```python
import functools

import jax
import jax.numpy as jnp
from jax import lax
from jax.experimental import pallas as pl
from jax.experimental.pallas import tpu as pltpu
from jax.sharding import PartitionSpec as P

TAPS = 128
FGROUP = 16
MODES = 16
CHUNK = 256
RING = 8
LANES = 128
MESH = pl.DeviceIdType.MESH
F32 = jnp.float32
BF16 = jnp.bfloat16


def dot(a, b):
    return lax.dot_general(a, b, (((1,), (0,)), ((), ())), preferred_element_type=F32)


def dot_t(a, b):
    return lax.dot_general(a, b, (((1,), (1,)), ((), ())), preferred_element_type=F32)


def split_float(values):
    high = values.astype(BF16)
    low = (values - high.astype(F32)).astype(BF16)
    return high, low


def iota(shape, axis):
    return lax.broadcasted_iota(jnp.int32, shape, axis)


def kernel(
    n_ctx,
    sq_hbm,
    sk_hbm,
    sv_hbm,
    lq_hbm,
    lk_hbm,
    taps_hbm,
    modes_hbm,
    out,
    sq,
    sk,
    sv,
    lq,
    lk,
    taps,
    modes,
    mixed,
    tails,
    halo,
    first,
    gates,
    added,
    relay,
    upper_w,
    taps_f,
    pad,
    fe,
    gt,
    filt,
    x,
    y,
    ends,
    from_z,
    z_out,
    z_in,
    a_out,
    a_in,
    b_out,
    b_in,
    v_in,
    load_sem,
    halo_send,
    halo_recv,
    z_send,
    z_recv,
    a_send,
    a_recv,
    b_send,
    b_recv,
    relay_send,
    relay_recv,
    v_send,
    v_recv,
    up,
    go,
    wrap,
    hand,
    up_near,
):
    chans, length = sk.shape
    half = length // 2
    groups = chans // FGROUP
    nz = n_ctx // RING
    me = lax.axis_index("ctx")
    plane = lax.div(me, RING)
    place = lax.rem(me, RING)
    after = lax.rem(me + 1, n_ctx)
    before = lax.rem(me + n_ctx - 1, n_ctx)

    def in_plane(k):
        return plane * RING + lax.rem(place + k, RING)

    def in_column(k):
        return lax.rem(plane + k, nz) * RING + place

    def load(n, src, dst):
        copy = pltpu.make_async_copy(src, dst, load_sem.at[n])
        copy.start()
        return copy

    tail_cols = ((half - TAPS, half), (length - TAPS, length))
    body_cols = ((0, half - TAPS), (half, length - TAPS))
    gate_cols = ((0, TAPS), (half, half + TAPS))
    rest_cols = ((TAPS, half), (half + TAPS, length))

    def load_pairs(n, pairs, columns):
        copies = []
        for lo, hi in columns:
            for src, dst in pairs:
                copies.append(load(n + len(copies), src.at[:, lo:hi], dst.at[:, lo:hi]))
        return copies

    mixed_pair = ((sk_hbm, sk), (sv_hbm, sv))
    gate_pair = ((sq_hbm, sq), (lk_hbm, lk))
    tail_loads = load_pairs(0, mixed_pair, tail_cols)
    gate_loads = load_pairs(4, gate_pair, gate_cols)
    modes_load = load(8, modes_hbm, modes)
    taps_load = load(9, taps_hbm, taps)
    body_loads = load_pairs(11, mixed_pair, body_cols)
    rest_loads = load_pairs(15, gate_pair, rest_cols)
    lq_load = load(10, lq_hbm, lq)

    hub = RING // 2 - 1
    border = nz - place
    both_true = jnp.logical_and
    negate = jnp.logical_not
    is_first = me == 0
    is_last = me == n_ctx - 1
    at_hub = place == hub
    inner_place = both_true(place >= 2, place < nz)
    at_relay = both_true(plane == 0, inner_place)
    top_edge = both_true(place == RING - 1, both_true(plane >= 1, plane < nz - 1))
    low_edge = both_true(place == 0, plane >= 2)
    edge = jnp.logical_or(top_edge, low_edge)
    low_hand = both_true(place == 0, both_true(plane >= 1, plane < nz - 1))

    is_late_column = both_true(lax.axis_index("chan") == 0, place == 0)
    is_late = both_true(is_late_column, plane == 0)
    is_known = []
    for k in range(1, nz):
        other = lax.rem(plane + k, nz)
        other_late = both_true(is_late_column, other == 0)
        known = jnp.logical_or(both_true(other < plane, negate(other_late)), is_late)
        is_known.append(known)
    entered = sum(known.astype(jnp.int32) for known in is_known)

    barrier = pltpu.get_barrier_semaphore()

    def signal(semaphore, device):
        pl.semaphore_signal(
            semaphore, inc=1, device_id={"ctx": device}, device_id_type=MESH
        )

    pl.when(negate(jnp.logical_or(is_first, low_edge)))(lambda: signal(barrier, before))
    pl.when(negate(jnp.logical_or(is_last, top_edge)))(lambda: signal(barrier, after))
    pl.when(negate(at_hub))(lambda: signal(barrier, plane * RING + hub))

    for k in range(1, nz):
        pl.when(negate(is_known[k - 1]))(
            functools.partial(signal, barrier, in_column(k))
        )

    @pl.when(at_relay)
    def _():
        signal(barrier, border * RING + RING - 1)
        signal(barrier, border * RING + RING)

    greetings = (
        negate(jnp.logical_or(is_first, low_edge)).astype(jnp.int32)
        + negate(jnp.logical_or(is_last, top_edge)).astype(jnp.int32)
        + jnp.where(at_hub, RING - 1, 0)
        + entered
        + edge.astype(jnp.int32)
    )

    modes_load.wait()
    taps_load.wait()
    rate = modes[0:groups, :]
    res = modes[groups : 2 * groups, :]
    taps_f[...] = taps[...].astype(F32)

    def spread(values):
        pad[...] = jnp.zeros_like(pad)
        pad[:, 0:MODES] = values
        return pltpu.roll(pad[...], 0, 1, stride=MODES, stride_axis=0)

    rate_row = jnp.sum(spread(rate), axis=0, keepdims=True)
    weight = spread(res * jnp.sqrt(rate))
    weight_row = jnp.sum(weight, axis=0, keepdims=True)
    steps = iota((CHUNK, LANES), 0).astype(F32)
    for h in range(2):
        r = rate_row[:, h * LANES : (h + 1) * LANES]
        high, low = split_float(jnp.exp(-r * steps))
        gt[h, :, 0:LANES] = high
        gt[h, :, LANES:] = low
        high, low = split_float(jnp.exp(-r * (CHUNK - 1.0 - steps)))
        fe[h, :, 0:LANES] = high
        fe[h, :, LANES:] = low

    total = jnp.zeros((groups, CHUNK), F32)
    for h in range(2):
        high, low = split_float(weight[:, h * LANES : (h + 1) * LANES])
        total = total + dot_t(jnp.concatenate([high, high], axis=1), gt[h])
        total = total + dot_t(
            jnp.concatenate([low, jnp.zeros_like(low)], axis=1), gt[h]
        )
    filt[...] = total

    for copy in tail_loads:
        copy.wait()
    for b, (lo, hi) in enumerate(tail_cols):
        product = sk[:, lo:hi] * sv[:, lo:hi]
        mixed[:, lo:hi] = product
        tails[b] = product
    pl.semaphore_wait(barrier, greetings)

    halo_copies = []
    for b, target in enumerate((after, before)):
        copy = pltpu.make_async_remote_copy(
            src_ref=tails.at[b],
            dst_ref=halo.at[b],
            send_sem=halo_send.at[b],
            recv_sem=halo_recv.at[b],
            device_id={"ctx": target},
            device_id_type=MESH,
        )
        halo_copies.append(copy)
    pl.when(negate(jnp.logical_or(is_last, top_edge)))(halo_copies[0].start)
    pl.when(negate(jnp.logical_or(is_first, low_edge)))(halo_copies[1].start)

    for k in range(1, nz):
        pl.when(is_known[nz - k - 1])(
            functools.partial(signal, up.at[k], in_column(nz - k))
        )

    pl.when(low_edge)(lambda: signal(up_near, in_column(nz - 1)))

    @pl.when(at_hub)
    def _():
        for k in range(1, RING):
            signal(go, in_plane(k))

    for copy in gate_loads:
        copy.wait()
    for b, (lo, hi) in enumerate(gate_cols):
        gates[b] = sq[:, lo:hi] * lk[:, lo:hi]

    def to_relay(n, source, device):
        return pltpu.make_async_remote_copy(
            src_ref=source,
            dst_ref=relay.at[n],
            send_sem=relay_send.at[n],
            recv_sem=relay_recv.at[n],
            device_id={"ctx": device},
            device_id_type=MESH,
        )

    top_device = lax.rem(nz - plane, nz)
    top_copies = [
        to_relay(0, tails.at[0], top_device),
        to_relay(1, gates.at[1], top_device),
    ]
    low_device = lax.rem(nz - plane + 1, nz)
    low_copies = [
        to_relay(2, gates.at[0], low_device),
        to_relay(3, tails.at[1], low_device),
    ]
    for copy in top_copies:
        pl.when(top_edge)(copy.start)
    for copy in low_copies:
        pl.when(low_edge)(copy.start)

    for copy in body_loads:
        copy.wait()
    for lo, hi in body_cols:
        mixed[:, lo:hi] = sk[:, lo:hi] * sv[:, lo:hi]
    for copy in rest_loads:
        copy.wait()

    lower_mask = iota((TAPS, TAPS), 1) >= iota((TAPS, TAPS), 0)
    blocks = length // TAPS
    firsts = (0, blocks // 2)

    def gated(rows, m, conv):
        cols = pl.ds(m * TAPS, TAPS)
        value = lk[rows, cols].astype(F32) * (sq[rows, cols].astype(F32) * conv)
        x[rows, cols] = value.astype(BF16)

    def short_group(g, _):
        rows = pl.ds(pl.multiple_of(g * FGROUP, FGROUP), FGROUP)
        line = jnp.broadcast_to(taps_f[pl.ds(g, 1), :], (TAPS, TAPS))
        skew = pltpu.roll(line, 0, 1, stride=1, stride_axis=0)
        upper = jnp.where(lower_mask, 0.0, skew).astype(BF16)
        lower = jnp.where(lower_mask, skew, 0.0).astype(BF16)
        upper_w[g] = upper
        data = []
        for m in range(blocks):
            if m in firsts:
                here = mixed[rows, m * TAPS : (m + 1) * TAPS]
                data.append(jnp.concatenate([jnp.zeros_like(here), here], axis=1))
            else:
                data.append(mixed[rows, (m - 1) * TAPS : (m + 1) * TAPS])
        short = dot(
            jnp.concatenate(data, axis=0), jnp.concatenate([upper, lower], axis=0)
        )
        for m in range(blocks):
            part = short[m * FGROUP : (m + 1) * FGROUP]
            if m in firsts:
                first[firsts.index(m), rows, :] = part
            gated(rows, m, part)
        return 0

    lax.fori_loop(0, groups, short_group, 0, unroll=4)

    diag = lax.div(iota((LANES, LANES), 0), FGROUP) == lax.div(
        iota((LANES, LANES), 1), MODES
    )

    def chunk_ends(chunk):
        for h in range(2):
            both = dot(
                x[h * LANES : (h + 1) * LANES, chunk * CHUNK : (chunk + 1) * CHUNK],
                fe[h],
            )
            own = jnp.where(diag, both[:, 0:LANES] + both[:, LANES:], 0.0)
            ends[chunk, :, h * LANES : (h + 1) * LANES] = jnp.sum(
                own.reshape(LANES // FGROUP, FGROUP, LANES), axis=0
            )

    for chunk in range(length // CHUNK):
        chunk_ends(chunk)

    chunk_decay = jnp.exp(-rate_row * float(CHUNK))
    powers = iota((RING, groups * MODES), 0).astype(F32)
    by_block = jnp.exp(-rate_row * (powers * half))
    powers = iota((nz, groups * MODES), 0).astype(F32)
    by_plane = jnp.exp(-rate_row * (powers * (half * RING)))

    def over_blocks(count):
        return jnp.exp(-rate_row * (half * count.astype(F32)))

    between = over_blocks(2 * n_ctx - 1 - 2 * me)

    def first_ends(values):
        parts = []
        for h in range(2):
            wide = dot(values[h * LANES : (h + 1) * LANES, :], fe[h, 0:TAPS, :])
            own = jnp.where(diag, wide[:, 0:LANES] + wide[:, LANES:], 0.0)
            parts.append(
                jnp.sum(own.reshape(LANES // FGROUP, FGROUP, LANES), axis=0)
            )
        return jnp.concatenate(parts, axis=1)

    def send(source, target, k, send_sem, recv_sem, device):
        return pltpu.make_async_remote_copy(
            src_ref=source,
            dst_ref=target.at[k],
            send_sem=send_sem.at[k],
            recv_sem=recv_sem.at[k],
            device_id={"ctx": device},
            device_id_type=MESH,
        )

    z_copies = []
    is_down = []
    is_early = []
    for k in range(1, nz):
        down = plane + k >= nz
        early = both_true(edge, down)
        if k == nz - 1:
            early = both_true(early, negate(low_edge))
        kind = jnp.where(down, jnp.where(early, 2, 1), 0)
        z_copies.append(send(z_out.at[kind], z_in, k, z_send, z_recv, in_column(k)))
        is_down.append(down)
        is_early.append(early)

    def block_ends():
        end_a = ends[0] * chunk_decay + ends[1]
        end_b = ends[2] * chunk_decay + ends[3]
        return end_a, end_b + end_a * between

    @pl.when(is_first)
    def _():
        halo[0] = jnp.zeros_like(halo[0])

    @pl.when(is_last)
    def _():
        halo[1] = tails[0]

    def add_halo(b):
        away = jnp.logical_or(both_true(b == 0, is_first), both_true(b == 1, is_last))
        copy = pltpu.make_async_remote_copy(
            src_ref=tails.at[b],
            dst_ref=halo.at[b],
            send_sem=halo_send.at[b],
            recv_sem=halo_recv.at[b],
            device_id={"ctx": after},
            device_id_type=MESH,
        )
        pl.when(negate(away))(copy.wait_recv)
        cols = pl.ds(pl.multiple_of(b * half, TAPS), TAPS)

        def group(g, _):
            rows = pl.ds(pl.multiple_of(g * FGROUP, FGROUP), FGROUP)
            extra = dot(halo[b, rows, :], upper_w[g])
            query = sq[rows, cols].astype(F32)
            key = lk[rows, cols].astype(F32)
            added[0, rows, :] = (key * (query * extra)).astype(BF16)
            x[rows, cols] = (key * (query * (extra + first[b, rows, :]))).astype(BF16)
            return 0

        lax.fori_loop(0, groups, group, 0, unroll=16)
        ends[2 * b] += first_ends(added[0])

    near = 1 - lax.rem(place, 2)
    add_halo(near)

    def start_column(k, wanted):
        @pl.when(wanted)
        def _():
            pl.when(negate(is_known[k - 1]))(lambda: pl.semaphore_wait(up.at[k], 1))
            z_copies[k - 1].start()

    @pl.when(edge)
    def _():
        z_out[2] = block_ends()[1].astype(BF16)
        for k in range(1, nz):
            start_column(k, both_true(is_early[k - 1], is_known[k - 1]))
        for k in range(1, nz):
            start_column(k, both_true(is_early[k - 1], negate(is_known[k - 1])))

    pl.when(low_hand)(lambda: pl.semaphore_wait(go, 1))

    @pl.when(low_hand)
    def _():
        pl.semaphore_wait(up_near, 1)
        signal(hand, in_column(1))

    @pl.when(low_edge)
    def _():
        pl.semaphore_wait(hand, 1)
        signal(wrap, before)
        halo_copies[1].start()

    @pl.when(top_edge)
    def _():
        pl.semaphore_wait(wrap, 1)
        halo_copies[0].start()

    add_halo(1 - near)
    end_a, both = block_ends()
    z_out[0] = end_a.astype(BF16)
    z_out[1] = both.astype(BF16)
    for k in range(1, nz):
        late = both_true(is_down[k - 1], negate(is_early[k - 1]))
        start_column(k, late)
    for k in range(1, nz):
        start_column(k, negate(is_down[k - 1]))

    def inner_group(g, _):
        rows = pl.ds(pl.multiple_of(g * FGROUP, FGROUP), FGROUP)
        line = jnp.broadcast_to(filt[pl.ds(g, 1), :], (TAPS, CHUNK))
        skew = pltpu.roll(line, 0, 1, stride=1, stride_axis=0)
        near = jnp.where(lower_mask, skew[:, 0:TAPS], 0.0).astype(BF16)
        far = skew[:, TAPS:].astype(BF16)
        table = jnp.concatenate(
            [
                jnp.concatenate([near, far], axis=1),
                jnp.concatenate([jnp.zeros_like(near), near], axis=1),
            ],
            axis=0,
        )
        chunks = length // CHUNK
        data = [x[rows, c * CHUNK : (c + 1) * CHUNK] for c in range(chunks)]
        inner = dot(jnp.concatenate(data, axis=0), table)
        for c in range(chunks):
            y[rows, c * CHUNK : (c + 1) * CHUNK] = inner[
                c * FGROUP : (c + 1) * FGROUP
            ]
        return 0

    lax.fori_loop(0, 6, inner_group, 0, unroll=3)

    relay_decay = over_blocks(
        jnp.maximum(RING * (border - plane) - 1 - place, 0)
    )

    def from_planes(first_half):
        from_z[...] = jnp.zeros_like(from_z)
        if not first_half:

            @pl.when(both_true(inner_place, plane < border))
            def _():
                pl.when(plane >= 1)(v_copies[0].wait_recv)
                from_z[...] += relay_decay * v_in[...].astype(F32)

        for k in reversed(range(1, nz)):
            power = k - 1 if first_half else nz - 1 - k

            @pl.when((plane >= k) if first_half else (plane < k))
            def _():
                z_copies[k - 1].wait_recv()
                from_z[...] += by_plane[power : power + 1] * z_in[k].astype(F32)

        return from_z[...]

    one_plane = by_plane[1:2]
    before_a = from_planes(True)
    a_out[0] = (before_a * one_plane + end_a).astype(BF16)
    a_out[1] = before_a.astype(BF16)
    a_copies = [
        send(a_out.at[lax.div(place + k, RING)], a_in, k, a_send, a_recv, in_plane(k))
        for k in range(1, RING)
    ]
    pl.when(negate(jnp.logical_or(at_hub, low_hand)))(
        lambda: pl.semaphore_wait(go, 1)
    )
    for copy in a_copies:
        copy.start()

    v_copies = [
        pltpu.make_async_remote_copy(
            src_ref=v_in,
            dst_ref=v_in,
            send_sem=v_send.at[k],
            recv_sem=v_recv,
            device_id={"ctx": in_column(k)},
            device_id_type=MESH,
        )
        for k in range(1, nz - 1)
    ]

    @pl.when(at_relay)
    def _():
        for n in range(4):
            to_relay(n, relay.at[n], top_device).wait_recv()

        def group(g, _):
            rows = pl.ds(pl.multiple_of(g * FGROUP, FGROUP), FGROUP)
            ended = jnp.concatenate([relay[0, rows, :], relay[3, rows, :]], axis=0)
            extra = dot(ended, upper_w[g])
            for b in range(2):
                part = extra[b * FGROUP : (b + 1) * FGROUP]
                gate = relay[2 - b, rows, :].astype(F32)
                added[b, rows, :] = (gate * part).astype(BF16)
            return 0

        lax.fori_loop(0, groups, group, 0, unroll=16)
        far = over_blocks(2 * RING * (place - 1))
        state = first_ends(added[1]) + first_ends(added[0]) * far
        v_in[...] = (state * chunk_decay).astype(BF16)
        for k in range(1, nz - 1):
            pl.when(k < border)(v_copies[k - 1].start)

    before_b = from_planes(False)
    b_out[0] = before_b.astype(BF16)
    b_out[1] = (before_b * one_plane + both).astype(BF16)
    b_copies = [
        send(b_out.at[lax.div(place + k, RING)], b_in, k, b_send, b_recv, in_plane(k))
        for k in range(1, RING)
    ]
    for copy in b_copies:
        copy.start()

    lax.fori_loop(6, groups, inner_group, 0, unroll=5)

    from_start = weight_row * jnp.exp(-rate_row)
    lq_load.wait()

    def finish(b, start):
        for h in range(2):
            lanes = slice(h * LANES, (h + 1) * LANES)
            rows = slice(h * LANES, (h + 1) * LANES)
            state = start[:, lanes]
            for c in range(2):
                chunk = 2 * b + c
                if c == 1:
                    state = state * chunk_decay[:, lanes] + ends[2 * b, :, lanes]
                scaled = state * from_start[:, lanes]
                tiled = jnp.concatenate([scaled] * (LANES // FGROUP), axis=0)
                states = jnp.where(diag, tiled, 0.0).astype(BF16)
                carried = dot_t(jnp.concatenate([states, states], axis=1), gt[h])
                cols = slice(chunk * CHUNK, (chunk + 1) * CHUNK)
                value = lq[rows, cols].astype(F32) * (y[rows, cols] + carried)
                out[rows, cols] = value.astype(BF16)

    start_a = before_a * by_block[RING - 1 : RING]
    for k in range(1, RING):
        a_copies[k - 1].wait_recv()
        start_a = start_a + by_block[k - 1 : k] * a_in[k].astype(F32)
    finish(0, start_a)

    start_b = before_b * by_block[RING - 1 : RING] + over_blocks(
        2 * n_ctx - 2 - 2 * me
    ) * (start_a * by_block[1:2] + end_a)
    for k in range(1, RING):
        b_copies[k - 1].wait_recv()
        start_b = start_b + by_block[RING - 1 - k : RING - k] * b_in[k].astype(F32)
    finish(1, start_b)

    pl.when(negate(is_last))(halo_copies[0].wait_send)
    pl.when(negate(is_first))(halo_copies[1].wait_send)
    for copy in top_copies:
        pl.when(top_edge)(copy.wait_send)
    for copy in low_copies:
        pl.when(low_edge)(copy.wait_send)
    for k in range(1, nz - 1):
        pl.when(both_true(at_relay, k < border))(v_copies[k - 1].wait_send)
    for copy in z_copies + a_copies + b_copies:
        copy.wait_send()


def per_device(sq, sk, sv, lq, lk, taps, res, rate):
    chans, length = sk.shape
    n_ctx = lax.axis_size("ctx")
    nz = n_ctx // RING
    groups = chans // FGROUP
    states = groups * MODES
    wide = pltpu.VMEM((chans, length), BF16)
    dma = pltpu.SemaphoreType.DMA
    scratch = [
        wide,
        wide,
        wide,
        wide,
        wide,
        pltpu.VMEM(taps.shape, BF16),
        pltpu.VMEM((2 * groups, MODES), F32),
        wide,
        pltpu.VMEM((2, chans, TAPS), BF16),
        pltpu.VMEM((2, chans, TAPS), BF16),
        pltpu.VMEM((2, chans, TAPS), F32),
        pltpu.VMEM((2, chans, TAPS), BF16),
        pltpu.VMEM((2, chans, TAPS), BF16),
        pltpu.VMEM((4, chans, TAPS), BF16),
        pltpu.VMEM((groups, TAPS, TAPS), BF16),
        pltpu.VMEM((groups, TAPS), F32),
        pltpu.VMEM((groups, states), F32),
        pltpu.VMEM((2, CHUNK, 2 * LANES), BF16),
        pltpu.VMEM((2, CHUNK, 2 * LANES), BF16),
        pltpu.VMEM((groups, CHUNK), F32),
        wide,
        pltpu.VMEM((chans, length), F32),
        pltpu.VMEM((length // CHUNK, FGROUP, states), F32),
        pltpu.VMEM((FGROUP, states), F32),
        pltpu.VMEM((3, FGROUP, states), BF16),
        pltpu.VMEM((nz, FGROUP, states), BF16),
        pltpu.VMEM((2, FGROUP, states), BF16),
        pltpu.VMEM((RING, FGROUP, states), BF16),
        pltpu.VMEM((2, FGROUP, states), BF16),
        pltpu.VMEM((RING, FGROUP, states), BF16),
        pltpu.VMEM((FGROUP, states), BF16),
        dma((19,)),
        dma((2,)),
        dma((2,)),
        dma((nz,)),
        dma((nz,)),
        dma((RING,)),
        dma((RING,)),
        dma((RING,)),
        dma((RING,)),
        dma((4,)),
        dma((4,)),
        dma((nz,)),
        dma(()),
        pltpu.SemaphoreType.REGULAR((nz,)),
        pltpu.SemaphoreType.REGULAR,
        pltpu.SemaphoreType.REGULAR,
        pltpu.SemaphoreType.REGULAR,
        pltpu.SemaphoreType.REGULAR,
    ]
    anywhere = pl.BlockSpec(memory_space=pl.ANY)
    modes = jnp.concatenate([rate, res], axis=0)
    return pl.pallas_call(
        functools.partial(kernel, n_ctx),
        out_shape=jax.ShapeDtypeStruct((chans, length), BF16),
        in_specs=[anywhere] * 7,
        out_specs=pl.BlockSpec(memory_space=pltpu.VMEM),
        scratch_shapes=scratch,
        compiler_params=pltpu.CompilerParams(
            collective_id=0, has_side_effects=True, vmem_limit_bytes=53 << 20
        ),
    )(sq, sk, sv, lq, lk, taps, modes)


def solution(mesh):
    in_specs = (P("chan", "ctx"),) * 5 + (P("chan", None),) * 3
    return jax.shard_map(
        per_device,
        mesh=mesh,
        in_specs=in_specs,
        out_specs=P("chan", "ctx"),
        check_vma=False,
    )
```

```python
import functools

import jax
import jax.numpy as jnp
from jax import lax
from jax.experimental import pallas as pl
from jax.experimental.pallas import tpu as pltpu
from jax.sharding import PartitionSpec as P

TAPS = 128
FGROUP = 16
MODES = 16
CHUNK = 256
RING = 8
LANES = 128
MESH = pl.DeviceIdType.MESH
F32 = jnp.float32
BF16 = jnp.bfloat16


def dot(a, b):
    return lax.dot_general(a, b, (((1,), (0,)), ((), ())), preferred_element_type=F32)


def dot_t(a, b):
    return lax.dot_general(a, b, (((1,), (1,)), ((), ())), preferred_element_type=F32)


def split_float(values):
    high = values.astype(BF16)
    low = (values - high.astype(F32)).astype(BF16)
    return high, low


def iota(shape, axis):
    return lax.broadcasted_iota(jnp.int32, shape, axis)


def kernel(
    n_ctx,
    sq_hbm,
    sk_hbm,
    sv_hbm,
    lq_hbm,
    lk_hbm,
    taps_hbm,
    modes_hbm,
    out,
    sq,
    sk,
    sv,
    lq,
    lk,
    taps,
    modes,
    mixed,
    tails,
    halo,
    first,
    gates,
    added,
    relay,
    upper_w,
    lower_w,
    taps_f,
    pad,
    fe,
    gt,
    filt,
    x,
    y,
    ends,
    from_z,
    z_out,
    z_in,
    a_out,
    a_in,
    b_out,
    b_in,
    v_in,
    load_sem,
    halo_send,
    halo_recv,
    z_send,
    z_recv,
    a_send,
    a_recv,
    b_send,
    b_recv,
    relay_send,
    relay_recv,
    v_send,
    v_recv,
    up,
    go,
    wrap,
    hand,
    up_near,
):
    chans, length = sk.shape
    half = length // 2
    groups = chans // FGROUP
    nz = n_ctx // RING
    me = lax.axis_index("ctx")
    plane = lax.div(me, RING)
    place = lax.rem(me, RING)
    after = lax.rem(me + 1, n_ctx)
    before = lax.rem(me + n_ctx - 1, n_ctx)

    def in_plane(k):
        return plane * RING + lax.rem(place + k, RING)

    def in_column(k):
        return lax.rem(plane + k, nz) * RING + place

    def load(n, src, dst):
        copy = pltpu.make_async_copy(src, dst, load_sem.at[n])
        copy.start()
        return copy

    tail_cols = ((half - TAPS, half), (length - TAPS, length))
    body_cols = ((0, half - TAPS), (half, length - TAPS))
    gate_cols = ((0, TAPS), (half, half + TAPS))
    rest_cols = ((TAPS, half), (half + TAPS, length))

    def load_pairs(n, pairs, columns):
        copies = []
        for lo, hi in columns:
            for src, dst in pairs:
                copies.append(load(n + len(copies), src.at[:, lo:hi], dst.at[:, lo:hi]))
        return copies

    mixed_pair = ((sk_hbm, sk), (sv_hbm, sv))
    gate_pair = ((sq_hbm, sq), (lk_hbm, lk))
    tail_loads = load_pairs(0, mixed_pair, tail_cols)
    gate_loads = load_pairs(4, gate_pair, gate_cols)
    modes_load = load(8, modes_hbm, modes)
    taps_load = load(9, taps_hbm, taps)
    block_loads = []
    for b in range(2):
        pairs = load_pairs(11 + 4 * b, mixed_pair, body_cols[b : b + 1])
        pairs += load_pairs(13 + 4 * b, gate_pair, rest_cols[b : b + 1])
        block_loads.append(pairs)
    lq_load = load(10, lq_hbm, lq)

    hub = RING // 2 - 1
    border = nz - place
    both_true = jnp.logical_and
    negate = jnp.logical_not
    is_first = me == 0
    is_last = me == n_ctx - 1
    at_hub = place == hub
    inner_place = both_true(place >= 2, place < nz)
    at_relay = both_true(plane == 0, inner_place)
    top_edge = both_true(place == RING - 1, both_true(plane >= 1, plane < nz - 1))
    low_edge = both_true(place == 0, plane >= 2)
    edge = jnp.logical_or(top_edge, low_edge)
    low_hand = both_true(place == 0, both_true(plane >= 1, plane < nz - 1))

    is_late_column = both_true(lax.axis_index("chan") == 0, place == 0)
    is_late = both_true(is_late_column, plane == 0)
    is_known = []
    for k in range(1, nz):
        other = lax.rem(plane + k, nz)
        other_late = both_true(is_late_column, other == 0)
        known = jnp.logical_or(both_true(other < plane, negate(other_late)), is_late)
        is_known.append(known)
    entered = sum(known.astype(jnp.int32) for known in is_known)

    barrier = pltpu.get_barrier_semaphore()

    def signal(semaphore, device):
        pl.semaphore_signal(
            semaphore, inc=1, device_id={"ctx": device}, device_id_type=MESH
        )

    pl.when(negate(jnp.logical_or(is_first, low_edge)))(lambda: signal(barrier, before))
    pl.when(negate(jnp.logical_or(is_last, top_edge)))(lambda: signal(barrier, after))
    pl.when(negate(at_hub))(lambda: signal(barrier, plane * RING + hub))

    for k in range(1, nz):
        pl.when(negate(is_known[k - 1]))(
            functools.partial(signal, barrier, in_column(k))
        )

    @pl.when(at_relay)
    def _():
        signal(barrier, border * RING + RING - 1)
        signal(barrier, border * RING + RING)

    greetings = (
        negate(jnp.logical_or(is_first, low_edge)).astype(jnp.int32)
        + negate(jnp.logical_or(is_last, top_edge)).astype(jnp.int32)
        + jnp.where(at_hub, RING - 1, 0)
        + entered
        + edge.astype(jnp.int32)
    )

    modes_load.wait()
    taps_load.wait()
    rate = modes[0:groups, :]
    res = modes[groups : 2 * groups, :]
    taps_f[...] = taps[...].astype(F32)

    def spread(values):
        pad[...] = jnp.zeros_like(pad)
        pad[:, 0:MODES] = values
        return pltpu.roll(pad[...], 0, 1, stride=MODES, stride_axis=0)

    rate_row = jnp.sum(spread(rate), axis=0, keepdims=True)
    weight = spread(res * jnp.sqrt(rate))
    weight_row = jnp.sum(weight, axis=0, keepdims=True)
    steps = iota((CHUNK, LANES), 0).astype(F32)
    for h in range(2):
        r = rate_row[:, h * LANES : (h + 1) * LANES]
        high, low = split_float(jnp.exp(-r * steps))
        gt[h, :, 0:LANES] = high
        gt[h, :, LANES:] = low
        high, low = split_float(jnp.exp(-r * (CHUNK - 1.0 - steps)))
        fe[h, :, 0:LANES] = high
        fe[h, :, LANES:] = low

    total = jnp.zeros((groups, CHUNK), F32)
    for h in range(2):
        high, low = split_float(weight[:, h * LANES : (h + 1) * LANES])
        total = total + dot_t(jnp.concatenate([high, high], axis=1), gt[h])
        total = total + dot_t(
            jnp.concatenate([low, jnp.zeros_like(low)], axis=1), gt[h]
        )
    filt[...] = total

    for copy in tail_loads:
        copy.wait()
    for b, (lo, hi) in enumerate(tail_cols):
        product = sk[:, lo:hi] * sv[:, lo:hi]
        mixed[:, lo:hi] = product
        tails[b] = product
    pl.semaphore_wait(barrier, greetings)

    halo_copies = []
    for b, target in enumerate((after, before)):
        copy = pltpu.make_async_remote_copy(
            src_ref=tails.at[b],
            dst_ref=halo.at[b],
            send_sem=halo_send.at[b],
            recv_sem=halo_recv.at[b],
            device_id={"ctx": target},
            device_id_type=MESH,
        )
        halo_copies.append(copy)
    pl.when(negate(jnp.logical_or(is_last, top_edge)))(halo_copies[0].start)
    pl.when(negate(jnp.logical_or(is_first, low_edge)))(halo_copies[1].start)

    for k in range(1, nz):
        pl.when(is_known[nz - k - 1])(
            functools.partial(signal, up.at[k], in_column(nz - k))
        )

    pl.when(low_edge)(lambda: signal(up_near, in_column(nz - 1)))

    @pl.when(at_hub)
    def _():
        for k in range(1, RING):
            signal(go, in_plane(k))

    for copy in gate_loads:
        copy.wait()
    for b, (lo, hi) in enumerate(gate_cols):
        gates[b] = sq[:, lo:hi] * lk[:, lo:hi]

    def to_relay(n, source, device):
        return pltpu.make_async_remote_copy(
            src_ref=source,
            dst_ref=relay.at[n],
            send_sem=relay_send.at[n],
            recv_sem=relay_recv.at[n],
            device_id={"ctx": device},
            device_id_type=MESH,
        )

    top_device = lax.rem(nz - plane, nz)
    top_copies = [
        to_relay(0, tails.at[0], top_device),
        to_relay(1, gates.at[1], top_device),
    ]
    low_device = lax.rem(nz - plane + 1, nz)
    low_copies = [
        to_relay(2, gates.at[0], low_device),
        to_relay(3, tails.at[1], low_device),
    ]
    for copy in top_copies:
        pl.when(top_edge)(copy.start)
    for copy in low_copies:
        pl.when(low_edge)(copy.start)

    lower_mask = iota((TAPS, TAPS), 1) >= iota((TAPS, TAPS), 0)
    blocks = length // TAPS
    firsts = (0, blocks // 2)

    def gated(rows, m, conv):
        cols = pl.ds(m * TAPS, TAPS)
        value = lk[rows, cols].astype(F32) * (sq[rows, cols].astype(F32) * conv)
        x[rows, cols] = value.astype(BF16)

    def short_group(b, g, _):
        rows = pl.ds(pl.multiple_of(g * FGROUP, FGROUP), FGROUP)
        if b == 0:
            line = jnp.broadcast_to(taps_f[pl.ds(g, 1), :], (TAPS, TAPS))
            skew = pltpu.roll(line, 0, 1, stride=1, stride_axis=0)
            upper = jnp.where(lower_mask, 0.0, skew).astype(BF16)
            lower = jnp.where(lower_mask, skew, 0.0).astype(BF16)
            upper_w[g] = upper
            lower_w[g] = lower
        else:
            upper = upper_w[g]
            lower = lower_w[g]
        begin = firsts[b]
        end = begin + blocks // 2
        here = mixed[rows, begin * TAPS : (begin + 1) * TAPS]
        data = [jnp.concatenate([jnp.zeros_like(here), here], axis=1)]
        for m in range(begin + 1, end):
            data.append(mixed[rows, (m - 1) * TAPS : (m + 1) * TAPS])
        short = dot(
            jnp.concatenate(data, axis=0), jnp.concatenate([upper, lower], axis=0)
        )
        for m in range(begin, end):
            part = short[(m - begin) * FGROUP : (m - begin + 1) * FGROUP]
            if m == begin:
                first[b, rows, :] = part
            gated(rows, m, part)
        return 0

    for b, (lo, hi) in enumerate(body_cols):
        for copy in block_loads[b]:
            copy.wait()
        mixed[:, lo:hi] = sk[:, lo:hi] * sv[:, lo:hi]
        lax.fori_loop(
            0, groups, functools.partial(short_group, b), 0, unroll=8
        )

    diag = lax.div(iota((LANES, LANES), 0), FGROUP) == lax.div(
        iota((LANES, LANES), 1), MODES
    )

    def chunk_ends(chunk):
        for h in range(2):
            both = dot(
                x[h * LANES : (h + 1) * LANES, chunk * CHUNK : (chunk + 1) * CHUNK],
                fe[h],
            )
            own = jnp.where(diag, both[:, 0:LANES] + both[:, LANES:], 0.0)
            ends[chunk, :, h * LANES : (h + 1) * LANES] = jnp.sum(
                own.reshape(LANES // FGROUP, FGROUP, LANES), axis=0
            )

    for chunk in range(length // CHUNK):
        chunk_ends(chunk)

    chunk_decay = jnp.exp(-rate_row * float(CHUNK))
    powers = iota((RING, groups * MODES), 0).astype(F32)
    by_block = jnp.exp(-rate_row * (powers * half))
    powers = iota((nz, groups * MODES), 0).astype(F32)
    by_plane = jnp.exp(-rate_row * (powers * (half * RING)))

    def over_blocks(count):
        return jnp.exp(-rate_row * (half * count.astype(F32)))

    between = over_blocks(2 * n_ctx - 1 - 2 * me)

    def first_ends(values):
        parts = []
        for h in range(2):
            wide = dot(values[h * LANES : (h + 1) * LANES, :], fe[h, 0:TAPS, :])
            own = jnp.where(diag, wide[:, 0:LANES] + wide[:, LANES:], 0.0)
            parts.append(
                jnp.sum(own.reshape(LANES // FGROUP, FGROUP, LANES), axis=0)
            )
        return jnp.concatenate(parts, axis=1)

    def send(source, target, k, send_sem, recv_sem, device):
        return pltpu.make_async_remote_copy(
            src_ref=source,
            dst_ref=target.at[k],
            send_sem=send_sem.at[k],
            recv_sem=recv_sem.at[k],
            device_id={"ctx": device},
            device_id_type=MESH,
        )

    z_copies = []
    is_down = []
    is_early = []
    for k in range(1, nz):
        down = plane + k >= nz
        early = both_true(edge, down)
        if k == nz - 1:
            early = both_true(early, negate(low_edge))
        kind = jnp.where(down, jnp.where(early, 2, 1), 0)
        z_copies.append(send(z_out.at[kind], z_in, k, z_send, z_recv, in_column(k)))
        is_down.append(down)
        is_early.append(early)

    def block_ends():
        end_a = ends[0] * chunk_decay + ends[1]
        end_b = ends[2] * chunk_decay + ends[3]
        return end_a, end_b + end_a * between

    @pl.when(is_first)
    def _():
        halo[0] = jnp.zeros_like(halo[0])

    @pl.when(is_last)
    def _():
        halo[1] = tails[0]

    def add_halo(b):
        away = jnp.logical_or(both_true(b == 0, is_first), both_true(b == 1, is_last))
        copy = pltpu.make_async_remote_copy(
            src_ref=tails.at[b],
            dst_ref=halo.at[b],
            send_sem=halo_send.at[b],
            recv_sem=halo_recv.at[b],
            device_id={"ctx": after},
            device_id_type=MESH,
        )
        pl.when(negate(away))(copy.wait_recv)
        cols = pl.ds(pl.multiple_of(b * half, TAPS), TAPS)

        def group(g, _):
            rows = pl.ds(pl.multiple_of(g * FGROUP, FGROUP), FGROUP)
            extra = dot(halo[b, rows, :], upper_w[g])
            query = sq[rows, cols].astype(F32)
            key = lk[rows, cols].astype(F32)
            added[0, rows, :] = (key * (query * extra)).astype(BF16)
            x[rows, cols] = (key * (query * (extra + first[b, rows, :]))).astype(BF16)
            return 0

        lax.fori_loop(0, groups, group, 0, unroll=16)
        ends[2 * b] += first_ends(added[0])

    near = 1 - lax.rem(place, 2)
    add_halo(near)

    def start_column(k, wanted):
        @pl.when(wanted)
        def _():
            pl.when(negate(is_known[k - 1]))(lambda: pl.semaphore_wait(up.at[k], 1))
            z_copies[k - 1].start()

    @pl.when(edge)
    def _():
        z_out[2] = block_ends()[1].astype(BF16)
        for k in range(1, nz):
            start_column(k, both_true(is_early[k - 1], is_known[k - 1]))
        for k in range(1, nz):
            start_column(k, both_true(is_early[k - 1], negate(is_known[k - 1])))

    pl.when(low_hand)(lambda: pl.semaphore_wait(go, 1))

    @pl.when(low_hand)
    def _():
        pl.semaphore_wait(up_near, 1)
        signal(hand, in_column(1))

    @pl.when(low_edge)
    def _():
        pl.semaphore_wait(hand, 1)
        signal(wrap, before)
        halo_copies[1].start()

    @pl.when(top_edge)
    def _():
        pl.semaphore_wait(wrap, 1)
        halo_copies[0].start()

    add_halo(1 - near)
    end_a, both = block_ends()
    z_out[0] = end_a.astype(BF16)
    z_out[1] = both.astype(BF16)
    for k in range(1, nz):
        late = both_true(is_down[k - 1], negate(is_early[k - 1]))
        start_column(k, late)
    for k in range(1, nz):
        start_column(k, negate(is_down[k - 1]))

    def inner_group(g, _):
        rows = pl.ds(pl.multiple_of(g * FGROUP, FGROUP), FGROUP)
        line = jnp.broadcast_to(filt[pl.ds(g, 1), :], (TAPS, CHUNK))
        skew = pltpu.roll(line, 0, 1, stride=1, stride_axis=0)
        near = jnp.where(lower_mask, skew[:, 0:TAPS], 0.0).astype(BF16)
        far = skew[:, TAPS:].astype(BF16)
        table = jnp.concatenate(
            [
                jnp.concatenate([near, far], axis=1),
                jnp.concatenate([jnp.zeros_like(near), near], axis=1),
            ],
            axis=0,
        )
        chunks = length // CHUNK
        data = [x[rows, c * CHUNK : (c + 1) * CHUNK] for c in range(chunks)]
        inner = dot(jnp.concatenate(data, axis=0), table)
        for c in range(chunks):
            y[rows, c * CHUNK : (c + 1) * CHUNK] = inner[
                c * FGROUP : (c + 1) * FGROUP
            ]
        return 0

    lax.fori_loop(0, 6, inner_group, 0, unroll=3)

    relay_decay = over_blocks(
        jnp.maximum(RING * (border - plane) - 1 - place, 0)
    )

    def from_planes(first_half):
        from_z[...] = jnp.zeros_like(from_z)
        if not first_half:

            @pl.when(both_true(inner_place, plane < border))
            def _():
                pl.when(plane >= 1)(v_copies[0].wait_recv)
                from_z[...] += relay_decay * v_in[...].astype(F32)

        for k in reversed(range(1, nz)):
            power = k - 1 if first_half else nz - 1 - k

            @pl.when((plane >= k) if first_half else (plane < k))
            def _():
                z_copies[k - 1].wait_recv()
                from_z[...] += by_plane[power : power + 1] * z_in[k].astype(F32)

        return from_z[...]

    one_plane = by_plane[1:2]
    before_a = from_planes(True)
    a_out[0] = (before_a * one_plane + end_a).astype(BF16)
    a_out[1] = before_a.astype(BF16)
    a_copies = [
        send(a_out.at[lax.div(place + k, RING)], a_in, k, a_send, a_recv, in_plane(k))
        for k in range(1, RING)
    ]
    pl.when(negate(jnp.logical_or(at_hub, low_hand)))(
        lambda: pl.semaphore_wait(go, 1)
    )
    for copy in a_copies:
        copy.start()

    v_copies = [
        pltpu.make_async_remote_copy(
            src_ref=v_in,
            dst_ref=v_in,
            send_sem=v_send.at[k],
            recv_sem=v_recv,
            device_id={"ctx": in_column(k)},
            device_id_type=MESH,
        )
        for k in range(1, nz - 1)
    ]

    @pl.when(at_relay)
    def _():
        for n in range(4):
            to_relay(n, relay.at[n], top_device).wait_recv()

        def group(g, _):
            rows = pl.ds(pl.multiple_of(g * FGROUP, FGROUP), FGROUP)
            ended = jnp.concatenate([relay[0, rows, :], relay[3, rows, :]], axis=0)
            extra = dot(ended, upper_w[g])
            for b in range(2):
                part = extra[b * FGROUP : (b + 1) * FGROUP]
                gate = relay[2 - b, rows, :].astype(F32)
                added[b, rows, :] = (gate * part).astype(BF16)
            return 0

        lax.fori_loop(0, groups, group, 0, unroll=16)
        far = over_blocks(2 * RING * (place - 1))
        state = first_ends(added[1]) + first_ends(added[0]) * far
        v_in[...] = (state * chunk_decay).astype(BF16)
        for k in range(1, nz - 1):
            pl.when(k < border)(v_copies[k - 1].start)

    before_b = from_planes(False)
    b_out[0] = before_b.astype(BF16)
    b_out[1] = (before_b * one_plane + both).astype(BF16)
    b_copies = [
        send(b_out.at[lax.div(place + k, RING)], b_in, k, b_send, b_recv, in_plane(k))
        for k in range(1, RING)
    ]
    for copy in b_copies:
        copy.start()

    lax.fori_loop(6, groups, inner_group, 0, unroll=5)

    from_start = weight_row * jnp.exp(-rate_row)
    lq_load.wait()

    def finish(b, start):
        for h in range(2):
            lanes = slice(h * LANES, (h + 1) * LANES)
            rows = slice(h * LANES, (h + 1) * LANES)
            state = start[:, lanes]
            for c in range(2):
                chunk = 2 * b + c
                if c == 1:
                    state = state * chunk_decay[:, lanes] + ends[2 * b, :, lanes]
                scaled = state * from_start[:, lanes]
                tiled = jnp.concatenate([scaled] * (LANES // FGROUP), axis=0)
                states = jnp.where(diag, tiled, 0.0).astype(BF16)
                carried = dot_t(jnp.concatenate([states, states], axis=1), gt[h])
                cols = slice(chunk * CHUNK, (chunk + 1) * CHUNK)
                value = lq[rows, cols].astype(F32) * (y[rows, cols] + carried)
                out[rows, cols] = value.astype(BF16)

    start_a = before_a * by_block[RING - 1 : RING]
    for k in range(1, RING):
        a_copies[k - 1].wait_recv()
        start_a = start_a + by_block[k - 1 : k] * a_in[k].astype(F32)
    finish(0, start_a)

    start_b = before_b * by_block[RING - 1 : RING] + over_blocks(
        2 * n_ctx - 2 - 2 * me
    ) * (start_a * by_block[1:2] + end_a)
    for k in range(1, RING):
        b_copies[k - 1].wait_recv()
        start_b = start_b + by_block[RING - 1 - k : RING - k] * b_in[k].astype(F32)
    finish(1, start_b)

    pl.when(negate(is_last))(halo_copies[0].wait_send)
    pl.when(negate(is_first))(halo_copies[1].wait_send)
    for copy in top_copies:
        pl.when(top_edge)(copy.wait_send)
    for copy in low_copies:
        pl.when(low_edge)(copy.wait_send)
    for k in range(1, nz - 1):
        pl.when(both_true(at_relay, k < border))(v_copies[k - 1].wait_send)
    for copy in z_copies + a_copies + b_copies:
        copy.wait_send()


def per_device(sq, sk, sv, lq, lk, taps, res, rate):
    chans, length = sk.shape
    n_ctx = lax.axis_size("ctx")
    nz = n_ctx // RING
    groups = chans // FGROUP
    states = groups * MODES
    wide = pltpu.VMEM((chans, length), BF16)
    dma = pltpu.SemaphoreType.DMA
    scratch = [
        wide,
        wide,
        wide,
        wide,
        wide,
        pltpu.VMEM(taps.shape, BF16),
        pltpu.VMEM((2 * groups, MODES), F32),
        wide,
        pltpu.VMEM((2, chans, TAPS), BF16),
        pltpu.VMEM((2, chans, TAPS), BF16),
        pltpu.VMEM((2, chans, TAPS), F32),
        pltpu.VMEM((2, chans, TAPS), BF16),
        pltpu.VMEM((2, chans, TAPS), BF16),
        pltpu.VMEM((4, chans, TAPS), BF16),
        pltpu.VMEM((groups, TAPS, TAPS), BF16),
        pltpu.VMEM((groups, TAPS, TAPS), BF16),
        pltpu.VMEM((groups, TAPS), F32),
        pltpu.VMEM((groups, states), F32),
        pltpu.VMEM((2, CHUNK, 2 * LANES), BF16),
        pltpu.VMEM((2, CHUNK, 2 * LANES), BF16),
        pltpu.VMEM((groups, CHUNK), F32),
        wide,
        pltpu.VMEM((chans, length), F32),
        pltpu.VMEM((length // CHUNK, FGROUP, states), F32),
        pltpu.VMEM((FGROUP, states), F32),
        pltpu.VMEM((3, FGROUP, states), BF16),
        pltpu.VMEM((nz, FGROUP, states), BF16),
        pltpu.VMEM((2, FGROUP, states), BF16),
        pltpu.VMEM((RING, FGROUP, states), BF16),
        pltpu.VMEM((2, FGROUP, states), BF16),
        pltpu.VMEM((RING, FGROUP, states), BF16),
        pltpu.VMEM((FGROUP, states), BF16),
        dma((19,)),
        dma((2,)),
        dma((2,)),
        dma((nz,)),
        dma((nz,)),
        dma((RING,)),
        dma((RING,)),
        dma((RING,)),
        dma((RING,)),
        dma((4,)),
        dma((4,)),
        dma((nz,)),
        dma(()),
        pltpu.SemaphoreType.REGULAR((nz,)),
        pltpu.SemaphoreType.REGULAR,
        pltpu.SemaphoreType.REGULAR,
        pltpu.SemaphoreType.REGULAR,
        pltpu.SemaphoreType.REGULAR,
    ]
    anywhere = pl.BlockSpec(memory_space=pl.ANY)
    modes = jnp.concatenate([rate, res], axis=0)
    return pl.pallas_call(
        functools.partial(kernel, n_ctx),
        out_shape=jax.ShapeDtypeStruct((chans, length), BF16),
        in_specs=[anywhere] * 7,
        out_specs=pl.BlockSpec(memory_space=pltpu.VMEM),
        scratch_shapes=scratch,
        compiler_params=pltpu.CompilerParams(
            collective_id=0, has_side_effects=True, vmem_limit_bytes=53 << 20
        ),
    )(sq, sk, sv, lq, lk, taps, modes)


def solution(mesh):
    in_specs = (P("chan", "ctx"),) * 5 + (P("chan", None),) * 3
    return jax.shard_map(
        per_device,
        mesh=mesh,
        in_specs=in_specs,
        out_specs=P("chan", "ctx"),
        check_vma=False,
    )
```
